256 devices in a mesh: grp: 8 (over z_hi, core), seq: 32 (over z_lo, y, x).
Axes of the slice: x: 4, y: 4, z: 8 (z_hi: 4, z_lo: 2; z = z_hi * 2 + z_lo), core: 2. Of those that a mesh axis runs over, the one named last changes fastest.
Arguments:
- query: bfloat16 [65536, 512], P(('grp', 'seq')), may hold values from -16 to 16
- key_in: bfloat16 [65536, 512], P(('grp', 'seq')), may hold values from -16 to 16
- value_in: bfloat16 [65536, 512], P(('grp', 'seq')), may hold values from -16 to 16
- grad_out: bfloat16 [65536, 512], P(('grp', 'seq')), may hold values from -6 to 6
Outputs:
- output: bfloat16 [65536, 512], P(('grp', 'seq'))
- grad_query: bfloat16 [65536, 512], P(('grp', 'seq'))
- grad_key: bfloat16 [65536, 512], P(('grp', 'seq'))
- grad_value: bfloat16 [65536, 512], P(('grp', 'seq'))
The draws below stay inside these ranges and needn't reach their ends.
All inputs are finite; a program needn't handle non-finite values.
Results may differ from the reference program's by a relative error of at most 0.018.
Values may be sent and summed in bfloat16 or wider, within the bound.
A program may use at most 128 MiB of HBM per device.

```python
from functools import partial
import jax
import jax.numpy as jnp
from jax import lax

H = 8
D = 512
BLK = 128
TOKENS = 65536


def layered(key, amplitude):
    total = jnp.zeros((TOKENS, D), jnp.float32)
    for number, grain in enumerate((3, 5, 7, 9, 11, 13, 15)):
        span = min(2 ** grain, TOKENS)
        sub_key = jax.random.fold_in(key, number)
        coarse = jax.random.truncated_normal(sub_key, -3.0, 3.0, (TOKENS // span, 1, D), jnp.float32)
        total = total + amplitude * jnp.broadcast_to(coarse, (TOKENS // span, span, D)).reshape(TOKENS, D)
    return total


def draw_query(key, part):
    key = jax.random.fold_in(key, 11)
    noise_key, layer_key = jax.random.split(key, 2)
    values = 1.2 * jax.random.truncated_normal(noise_key, -3.0, 3.0, (TOKENS, D), jnp.float32) + layered(layer_key, 0.45)
    return values.astype(jnp.bfloat16)


def draw_key_in(key, part):
    key = jax.random.fold_in(key, 23)
    noise_key, layer_key = jax.random.split(key, 2)
    values = 1.2 * jax.random.truncated_normal(noise_key, -3.0, 3.0, (TOKENS, D), jnp.float32) + layered(layer_key, 0.45)
    return values.astype(jnp.bfloat16)


def draw_value_in(key, part):
    key = jax.random.fold_in(key, 37)
    noise_key, layer_key = jax.random.split(key, 2)
    values = jax.random.truncated_normal(noise_key, -3.0, 3.0, (TOKENS, D), jnp.float32) + layered(layer_key, 0.45)
    return values.astype(jnp.bfloat16)


def steps_of(stream_key, extent, cuts, least, top_value):
    loudness, own = 1.0, jax.random.fold_in(stream_key, 6)
    for dim, blocks in cuts:
        heights = jnp.exp(jax.random.uniform(jax.random.fold_in(own, dim), (blocks,), jnp.float32, least / len(cuts), top_value / len(cuts)))
        loudness = loudness * jnp.repeat(heights, extent[dim] // blocks).reshape([-1 if axis == dim else 1 for axis in range(len(extent))])
    return loudness


def normal_values(own_key, extent, deviation, reach, cuts=(), dtype=jnp.bfloat16):
    loudness = steps_of(own_key, extent, cuts, -0.22, 0.18) if cuts else 1.0
    drawn = jax.random.normal(own_key, extent, jnp.float32) * deviation * loudness
    return jnp.minimum(jnp.maximum(drawn, -reach), reach).astype(dtype)


def setup_inputs(seed: int = 0) -> dict:
    key_of = jax.random.split(jax.random.key(seed), 5)
    query = draw_query(jax.random.fold_in(key_of[4], 71), 0)
    key_in = draw_key_in(jax.random.fold_in(key_of[4], 71), 0)
    value_in = draw_value_in(jax.random.fold_in(key_of[4], 71), 0)
    grad_out = normal_values(key_of[3], (TOKENS, D), 1.0, 6.0, ((0, 256),))
    return {"query": query, "key_in": key_in, "value_in": value_in, "grad_out": grad_out}


HIGH = lax.Precision.HIGHEST


def to_bf16(values):
    return lax.optimization_barrier(values.astype(jnp.bfloat16))


def coarsen(values):
    count, width = values.shape
    pairs = values.astype(jnp.float32).reshape(count // 2, 2, width)
    return to_bf16((pairs[:, 0] + pairs[:, 1]) * 0.5)


def spread(values, factor):
    count = values.shape[0]
    wide = jnp.broadcast_to(values[:, None], (count, factor) + values.shape[1:])
    return wide.reshape((count * factor,) + values.shape[1:])


def collapse(values, factor):
    count = values.shape[0] // factor
    return jnp.sum(values.reshape((count, factor) + values.shape[1:]), axis=1)


def level_forward(q_rows, keys, vals, scale):
    scores = jnp.einsum("prhe,pche->prhc", q_rows.astype(jnp.float32), keys.astype(jnp.float32), precision=HIGH) * scale
    peak = jnp.max(scores, axis=3)
    lifted = jnp.exp(scores - peak[..., None])
    total = jnp.sum(lifted, axis=3)
    weights = to_bf16(lifted).astype(jnp.float32)
    weighted = jnp.einsum("prhc,pche->prhe", weights, vals.astype(jnp.float32), precision=HIGH)
    return peak, total, weighted


def level_backward(q_rows, keys, vals, peak, grad_weighted, grad_total, scale):
    q_wide = q_rows.astype(jnp.float32)
    keys_wide = keys.astype(jnp.float32)
    vals_wide = vals.astype(jnp.float32)
    scores = jnp.einsum("prhe,pche->prhc", q_wide, keys_wide, precision=HIGH) * scale
    lifted = jnp.exp(scores - peak[..., None])
    weights = to_bf16(lifted).astype(jnp.float32)
    grad_wide = grad_weighted.astype(jnp.float32)
    grad_vals = jnp.einsum("prhc,prhe->pche", weights, grad_wide, precision=HIGH)
    grad_lift = jnp.einsum("prhe,pche->prhc", grad_wide, vals_wide, precision=HIGH)
    grad_scores = to_bf16(lifted * (grad_lift + grad_total[..., None])).astype(jnp.float32)
    grad_rows = jnp.einsum("prhc,pche->prhe", grad_scores, keys_wide, precision=HIGH) * scale
    grad_keys = jnp.einsum("prhc,prhe->pche", grad_scores, q_wide, precision=HIGH) * scale
    return grad_rows, grad_keys, grad_vals


def stretched(function, arrays, count):
    group = min(count, 16)
    shaped = tuple(item.reshape((count // group, group) + item.shape[1:]) for item in arrays)
    result = lax.map(lambda items: function(*items), shaped)
    return tuple(part_out.reshape((count,) + part_out.shape[2:]) for part_out in result)


def pair_flip(values, blocks, heads, depth):
    return values.reshape(blocks // 2, 2, BLK, heads, depth)[:, ::-1].reshape(blocks, BLK, heads, depth)


def level_blocks(q_lvl, k_lvl, v_lvl, level, heads, depth):
    count = q_lvl.shape[0]
    if level == 0:
        pairs = count // (2 * BLK)
        shape = (pairs, 2 * BLK, heads, depth)
        return q_lvl.reshape(shape), k_lvl.reshape(shape), v_lvl.reshape(shape), pairs
    blocks = count // BLK
    shape = (blocks, BLK, heads, depth)
    return q_lvl.reshape(shape), pair_flip(k_lvl, blocks, heads, depth), pair_flip(v_lvl, blocks, heads, depth), blocks


def reference(query, key_in, value_in, grad_out):
    tokens, width = query.shape
    heads = H
    depth = width // heads
    scale = depth ** -0.5
    levels = (tokens // BLK).bit_length() - 1
    queries = [query]
    key_rows = [key_in]
    value_rows = [value_in]
    for level in range(1, levels):
        queries.append(coarsen(queries[-1]))
        key_rows.append(coarsen(key_rows[-1]))
        value_rows.append(coarsen(value_rows[-1]))
    saved = []
    peaks = []
    totals = []
    weighted_rows = []
    for level in range(levels):
        q_blk, k_blk, v_blk, count = level_blocks(queries[level], key_rows[level], value_rows[level], level, heads, depth)
        peak, total, weighted = stretched(partial(level_forward, scale=scale), (q_blk, k_blk, v_blk), count)
        size = queries[level].shape[0]
        peaks.append(peak.reshape(size, heads))
        totals.append(total.reshape(size, heads))
        weighted_rows.append(weighted.reshape(size, heads, depth))
        saved.append((q_blk, k_blk, v_blk, count, peak))
    crest = spread(peaks[0], 1)
    for level in range(1, levels):
        crest = jnp.maximum(crest, spread(peaks[level], 2 ** level))
    numer = jnp.zeros((tokens, heads, depth), jnp.float32)
    denom = jnp.zeros((tokens, heads), jnp.float32)
    shares = []
    for level in range(levels):
        factor = 2 ** level
        share = (2.0 ** level) * jnp.exp(spread(peaks[level], factor) - crest)
        shares.append(share)
        numer = numer + share[..., None] * spread(weighted_rows[level], factor)
        denom = denom + share * spread(totals[level], factor)
    ratio = numer / denom[..., None]
    output = ratio.reshape(tokens, width).astype(jnp.bfloat16)
    upstream = grad_out.astype(jnp.float32).reshape(tokens, heads, depth)
    scaled = upstream / denom[..., None]
    drift = -jnp.sum(upstream * ratio, axis=2) / denom
    grads_q = []
    grads_k = []
    grads_v = []
    for level in range(levels):
        factor = 2 ** level
        q_blk, k_blk, v_blk, count, peak = saved[level]
        grad_weighted = to_bf16(collapse(shares[level][..., None] * scaled, factor))
        grad_total = collapse(shares[level] * drift, factor)
        grad_weighted = grad_weighted.reshape(q_blk.shape)
        grad_total = grad_total.reshape(peak.shape)
        grad_rows, grad_keys, grad_vals = stretched(partial(level_backward, scale=scale), (q_blk, k_blk, v_blk, peak, grad_weighted, grad_total), count)
        size = queries[level].shape[0]
        if level > 0:
            grad_keys = pair_flip(grad_keys, count, heads, depth)
            grad_vals = pair_flip(grad_vals, count, heads, depth)
        grads_q.append(grad_rows.reshape(size, width))
        grads_k.append(grad_keys.reshape(size, width))
        grads_v.append(grad_vals.reshape(size, width))
    running_q = grads_q[levels - 1]
    running_k = grads_k[levels - 1]
    running_v = grads_v[levels - 1]
    for level in reversed(range(levels - 1)):
        running_q = spread(running_q, 2) * 0.5 + grads_q[level]
        running_k = spread(running_k, 2) * 0.5 + grads_k[level]
        running_v = spread(running_v, 2) * 0.5 + grads_v[level]
    return output, running_q.astype(jnp.bfloat16), running_k.astype(jnp.bfloat16), running_v.astype(jnp.bfloat16)
```

```python
import functools

import jax
import jax.numpy as jnp
from jax import lax
from jax.experimental import pallas as pl
from jax.experimental.pallas import tpu as pltpu
from jax.sharding import PartitionSpec as P

MESH = pl.DeviceIdType.MESH
F32 = jnp.float32
BF16 = jnp.bfloat16
LANES = 128
NT = (((1,), (1,)), ((), ()))
TN = (((0,), (0,)), ((), ()))


def flip(value, mask, bits):
    out = 0
    for bit in range(bits):
        own = (value // 2**bit) % 2
        if isinstance(mask, int):
            out = out + 2**bit * (1 - own if (mask >> bit) & 1 else own)
        else:
            out = out + 2**bit * ((own + (mask // 2**bit) % 2) % 2)
    return out


def iota(shape, dim):
    return lax.broadcasted_iota(jnp.int32, shape, dim)


def shr(value, amount):
    return jnp.right_shift(value, amount)


def mm(a, b):
    return jnp.dot(a, b, preferred_element_type=F32)


def mm_nt(a, b):
    return lax.dot_general(a, b, NT, preferred_element_type=F32)


def mm_tn(a, b):
    return lax.dot_general(a, b, TN, preferred_element_type=F32)


def pool_matrix(rows, weight=0.5):
    shape = (rows // 2, rows)
    return jnp.where(shr(iota(shape, 1), 1) == iota(shape, 0), weight, 0.0).astype(BF16)


def spread_matrix(rows, weight):
    shape = (2 * rows, rows)
    return jnp.where(shr(iota(shape, 0), 1) == iota(shape, 1), weight, 0.0).astype(BF16)


def coarsen(values):
    return mm(pool_matrix(values.shape[0]), values).astype(BF16)


def lane_low():
    return iota((1, LANES), 1) < 64


def head_masks(weight):
    low = lane_low()
    return (
        jnp.where(low, weight, 0.0).astype(BF16),
        jnp.where(low, 0.0, weight).astype(BF16),
    )


def with_ones(vals):
    return jnp.concatenate([vals, jnp.ones_like(vals)], axis=1)


def fold(stacked, rows):
    return jnp.where(lane_low(), stacked[:rows], stacked[rows:])


def split2(values):
    high = values.astype(BF16)
    return high, (values - high.astype(F32)).astype(BF16)


def stack_heads(q):
    low, high = head_masks(0.125)
    return jnp.concatenate([q * low, q * high], axis=0)


def soft_weights(scores):
    peak = jnp.max(scores, axis=1, keepdims=True).astype(BF16).astype(F32)
    return jnp.exp(scores - peak).astype(BF16), peak


def attend(q, kv):
    rows = q.shape[0]
    scores = mm_nt(stack_heads(q), kv[:, :LANES])
    weights, peak = soft_weights(scores)
    both = mm(weights, with_ones(kv[:, LANES:]))
    weighted = fold(both[:, :LANES], rows)
    total = fold(both[:, LANES:], rows)
    wide = jnp.broadcast_to(peak, (2 * rows, LANES))
    return weights, fold(wide, rows), weighted, total


def stack_grads(gw, gt):
    low, high = head_masks(1.0)
    lane = iota((1, LANES), 1)
    first = jnp.where((lane == 0) | (lane == 64), 1.0, 0.0).astype(BF16)
    second = jnp.where((lane == 1) | (lane == 65), 1.0, 0.0).astype(BF16)
    gt_high, gt_low = split2(gt)
    extra = gt_high * first + gt_low * second
    return jnp.concatenate(
        [
            jnp.concatenate([gw * low, extra * low], axis=1),
            jnp.concatenate([gw * high, extra * high], axis=1),
        ],
        axis=0,
    )


def attend_back(q, kv, weights, gw, gt):
    rows = q.shape[0]
    stacked = stack_grads(gw, gt)
    lift = mm_nt(stacked, with_ones(kv[:, LANES:]))
    gs = (weights.astype(F32) * lift).astype(BF16)
    gv = mm_tn(weights, stacked[:, :LANES])
    gk = mm_tn(gs, stack_heads(q))
    gq = fold(mm(gs, kv[:, :LANES]), rows) * 0.125
    return gq, jnp.concatenate([gk, gv], axis=1)


OFFS = (0, 64, 96, 112, 120)


def row_level(row):
    level = jnp.zeros_like(row)
    for edge in OFFS[1:]:
        level = level + jnp.where(row >= edge, 1, 0)
    return level


def pick(full, level, width=LANES):
    out = jnp.where(level == 0, full[:, :width], 0.0)
    for index in range(1, 5):
        out = jnp.where(level == index, full[:, index * width : (index + 1) * width], out)
    return out


def blocks_of(values, level):
    zero = jnp.zeros_like(values)
    return jnp.concatenate([jnp.where(level == i, values, zero) for i in range(5)], axis=1)


def level_spread():
    parts = []
    shape = (LANES, LANES)
    row, col = iota(shape, 0), iota(shape, 1)
    for index, start in enumerate(OFFS):
        parts.append(jnp.where(col == start + shr(row, index + 1), 1.0, 0.0))
    return parts


def level_pool():
    parts = []
    shape = (LANES, LANES)
    row, col = iota(shape, 0), iota(shape, 1)
    for index, start in enumerate(OFFS):
        parts.append(jnp.where(row == start + shr(col, index + 1), 1.0, 0.0))
    return jnp.concatenate(parts, axis=1).astype(BF16)


def kernel(
    q_ref, k_ref, v_ref, g_ref, out_ref, gq_ref, gk_ref, gv_ref,
    qb, kvb, gb, l3, l4, kv3own, kv3sib, r4, own5, own6, own7, own8, rf,
    qp, kvp, w0, w1, w0w, w0p, w0t, w1w, w1p, w1t,
    a1, b1, m1, n1, d1, gw0, gt0, gw1, gt1, spm, spn, spd, g1s, d1s, g2s, d2s,
    ob, oq, bk, bkr, gq1, gkv1, gkv2, sb, rb, t4, m3s, m4s, cb, g4s,
    p_send, p_recv, a_send, a_recv, b_send, b_recv, bb_send, bb_recv, aa_send, aa_recv,
    o_send, o_recv, loc,
):
    grp, seq = lax.axis_index("grp"), lax.axis_index("seq")
    x, y = seq % 4, (seq // 4) % 4
    w = grp * 2 + seq // 16
    y_pair, y_bit = y // 2, y % 2
    sib = flip(y, 1, 2)

    def place(px, py, pw):
        return (pw // 2, (pw % 2) * 16 + py * 4 + px)

    def remote(src, dst, send, recv, device):
        return pltpu.make_async_remote_copy(
            src_ref=src, dst_ref=dst, send_sem=send, recv_sem=recv,
            device_id=device, device_id_type=MESH,
        )

    plane = [(mx, my) for my in (1, 2, 3, 0) for mx in range(4) if (mx, my) != (0, 0)]

    barrier = pltpu.get_barrier_semaphore()
    for mx, my in plane:
        pl.semaphore_signal(
            barrier, inc=1, device_id=place(flip(x, mx, 2), flip(y, my, 2), w), device_id_type=MESH
        )
    for m in range(1, 16):
        pl.semaphore_signal(
            barrier, inc=1, device_id=place(x, y, flip(w, m, 4)), device_id_type=MESH
        )

    for part, ref in ((0, k_ref), (1, v_ref)):
        rows = coarsen(coarsen(coarsen(ref[...])))
        upper = coarsen(rows)
        for j in range(4):
            l3[j, :, part * LANES : (part + 1) * LANES] = rows[:, j * LANES : (j + 1) * LANES]
            l4[j, :, part * LANES : (part + 1) * LANES] = upper[:, j * LANES : (j + 1) * LANES]

    pl.semaphore_wait(barrier, 30)

    stage_a = []
    for index, (mx, my) in enumerate(plane):
        px, py = flip(x, mx, 2), flip(y, my, 2)
        if my == 0:
            src, dst = l3.at[px], kv3own.at[x]
        elif my == 1:
            src, dst = l3.at[px], kv3sib.at[x]
        else:
            src, dst = l4.at[px], r4.at[y, x]
        copy = remote(src, dst, a_send.at[index], a_recv.at[index], place(px, py, w))
        copy.start()
        stage_a.append(copy)

    def lanes(index):
        return pl.ds(pl.multiple_of(index * LANES, LANES), LANES)

    def token_copies(mask):
        px = flip(x, mask, 2)
        device = place(px, y, w)
        pairs = (
            (k_ref, kvb.at[x, :, pl.ds(0, LANES)]),
            (v_ref, kvb.at[x, :, pl.ds(LANES, LANES)]),
            (q_ref, qb.at[x]),
            (g_ref, gb.at[x]),
        )
        return [
            remote(
                ref.at[:, lanes(px)], dst, p_send.at[i, mask - 1], p_recv.at[i, mask - 1], device
            )
            for i, (ref, dst) in enumerate(pairs)
        ]

    moves = [token_copies(mask) for mask in (1, 2, 3)]
    for i in range(4):
        for copies in moves:
            copies[i].start()

    kvb[x, :, :LANES] = k_ref[:, lanes(x)]
    kvb[x, :, LANES:] = v_ref[:, lanes(x)]
    qb[x] = q_ref[:, lanes(x)]
    gb[x] = g_ref[:, lanes(x)]
    kv3own[x] = l3[x]

    def chunk_forward(slot):
        q, kv = qb[slot], kvb[slot]
        weights, peak, weighted, total = attend(q, kv)
        w0[slot] = weights
        w0p[slot], w0w[slot], w0t[slot] = peak, weighted, total
        qp[slot] = coarsen(q)
        kvp[slot] = coarsen(kv)

    chunk_forward(x)

    for copy in stage_a:
        copy.wait_recv()
    half = pool_matrix(LANES)
    r4[y] = mm(half, kv3own[...].reshape(LANES, 256)).astype(BF16).reshape(4, 16, 256)
    r4[sib] = mm(half, kv3sib[...].reshape(LANES, 256)).astype(BF16).reshape(4, 16, 256)
    kvp[7] = kv3sib[...].reshape(LANES, 256)
    rows5 = coarsen(r4[...].reshape(256, 256))
    rows6 = coarsen(rows5)
    rows7 = coarsen(rows6)
    rows8 = coarsen(rows7)
    own5[...] = rows5.reshape(8, 16, 256)
    own6[...] = rows6.reshape(4, 16, 256)
    own7[...] = rows7.reshape(2, 16, 256)
    own8[...] = rows8.reshape(1, 16, 256)

    stage_b = []
    owns = (own5, own6, own7, own8)
    for m in range(1, 16):
        up = m.bit_length() - 1
        count = 8 >> up
        start = 8 * up + (w % 2**up) * count
        copy = remote(
            owns[up], rf.at[pl.ds(start, count)], b_send.at[m - 1], b_recv.at[m - 1],
            place(x, y, flip(w, m, 4)),
        )
        copy.start()
        stage_b.append(copy)

    def chunk_step(mask, carry):
        px = flip(x, mask, 2)
        for copy in token_copies(mask)[:3]:
            copy.wait_recv()
        chunk_forward(px)
        return carry

    lax.fori_loop(1, 4, chunk_step, 0)

    qp[4] = coarsen(qp[0:2].reshape(256, LANES))
    qp[5] = coarsen(qp[2:4].reshape(256, LANES))
    kvp[4] = coarsen(kvp[0:2].reshape(256, 256))
    kvp[5] = coarsen(kvp[2:4].reshape(256, 256))
    qp[6] = coarsen(qp[4:6].reshape(256, LANES))

    def unit_step(unit, carry):
        other = unit + 1 - 2 * (unit % 2)
        weights, peak, weighted, total = attend(qp[unit], kvp[other])
        w1[unit] = weights
        w1p[unit], w1w[unit], w1t[unit] = peak, weighted, total
        return carry

    lax.fori_loop(0, 7, unit_step, 0)

    qs = mm(half, qp[6])
    qs = jnp.concatenate([qs, jnp.zeros((64, LANES), F32)], axis=0)
    shape = (LANES, LANES)
    row, col = iota(shape, 0), iota(shape, 1)
    down = jnp.where((row >= 64) & (shr(col, 1) == row - 64), 0.5, 0.0).astype(BF16)
    qs = qs.astype(BF16)
    upper_rows = iota((LANES, 1), 0) >= 64
    for _ in range(4):
        qs = jnp.where(upper_rows, mm(down, qs), qs.astype(F32)).astype(BF16)
    level = row_level(jnp.bitwise_and(iota((256, 1), 0), 127))

    for copy in stage_b:
        copy.wait_recv()
    far4 = r4[pl.ds(2 * (1 - y_pair), 2)].reshape(LANES, 256)
    far = jnp.concatenate([far4, rf[...].reshape(512, 256)], axis=0)
    far_vals = with_ones(far[:, LANES:])
    q_stack = stack_heads(qs)
    weights_s, peak_s = soft_weights(pick(mm_nt(q_stack, far[:, :LANES]), level))
    blocks_s = blocks_of(weights_s, level)
    both = mm(blocks_s, far_vals)
    weighted_s = fold(both[:, :LANES], LANES)
    total_s = fold(both[:, LANES:], LANES)
    peak_s = fold(jnp.broadcast_to(peak_s, (256, LANES)), LANES)

    spreads = level_spread()
    stats = jnp.concatenate(
        [peak_s.astype(BF16), *split2(weighted_s), *split2(total_s)], axis=1
    )
    taken = [mm(part.astype(BF16), stats) for part in spreads]
    m3 = w1p[6]
    for t in taken:
        m3 = jnp.maximum(m3, t[:, :LANES])
    a3 = jnp.exp(w1p[6] - m3)
    n3, d3 = a3 * w1w[6], a3 * w1t[6]
    shares_s = []
    for index, t in enumerate(taken):
        share = 2.0 ** (index + 1) * jnp.exp(t[:, :LANES] - m3)
        n3 = n3 + share * (t[:, 128:256] + t[:, 256:384])
        d3 = d3 + share * (t[:, 384:512] + t[:, 512:640])
        shares_s.append(share)

    def doubled(ref, values, count):
        ref[pl.ds(0, count, 2), :] = values
        ref[pl.ds(1, count, 2), :] = values
        return ref[0 : 2 * count, :]

    def paired(ref, values, count):
        ref[0:count, :] = values
        return ref[pl.ds(0, count // 2, 2), :] + ref[pl.ds(1, count // 2, 2), :]

    def merge(peak, weighted, total, m, n, d):
        crest = jnp.maximum(peak, m)
        own = jnp.exp(peak - crest)
        rest = 2.0 * jnp.exp(m - crest)
        return crest, own * weighted + rest * n, own * total + rest * d, own, rest

    m2, n2, d2, own2, rest2 = merge(
        w1p[4:6].reshape(256, LANES), w1w[4:6].reshape(256, LANES), w1t[4:6].reshape(256, LANES),
        doubled(spm, m3, 128), doubled(spn, n3, 128), doubled(spd, d3, 128),
    )
    crest1, n1v, d1v, own1, rest1 = merge(
        w1p[0:4].reshape(512, LANES), w1w[0:4].reshape(512, LANES), w1t[0:4].reshape(512, LANES),
        doubled(spm, m2, 256), doubled(spn, n2, 256), doubled(spd, d2, 256),
    )
    m1[...] = crest1.reshape(4, LANES, LANES)
    n1[...] = n1v.reshape(4, LANES, LANES)
    d1[...] = d1v.reshape(4, LANES, LANES)
    a1[...], b1[...] = own1, rest1

    same = jnp.where(shr(iota(shape, 0), 6) == shr(iota(shape, 1), 6), 1.0, 0.0).astype(BF16)
    head_sum = jnp.concatenate([same, same], axis=0)

    def output_copy(kind, mask):
        px = flip(x, mask, 2)
        if kind == 0:
            src, dst = ob.at[px], out_ref.at[:, lanes(x)]
        elif kind == 1:
            src, dst = oq.at[px], gq_ref.at[:, lanes(x)]
        else:
            src, dst = bk.at[px], bkr.at[x]
        return remote(
            src, dst, o_send.at[kind, mask - 1], o_recv.at[kind, mask - 1], place(px, y, w)
        )

    def merge_step(mask, carry):
        px = flip(x, mask, 2)

        @pl.when(mask < 4)
        def _():
            token_copies(mask)[3].wait_recv()

        crest, numer, denom, own, rest = merge(
            w0p[px], w0w[px], w0t[px],
            doubled(spm, m1[px], 128), doubled(spn, n1[px], 128), doubled(spd, d1[px], 128),
        )
        ratio = numer / denom
        ob[px] = ratio.astype(BF16)
        up = gb[px].astype(F32)
        high, low = split2(up * ratio)
        inverse = 1.0 / denom
        drift = -mm(jnp.concatenate([high, low], axis=1), head_sum) * inverse
        scaled = up * inverse
        gw0[px] = (own * scaled).astype(BF16)
        gt0[px] = own * drift
        g1s[px] = paired(spm, rest * scaled, 256)
        d1s[px] = paired(spn, rest * drift, 256)

        @pl.when(mask < 4)
        def _():
            output_copy(0, mask).start()

        return carry

    lax.fori_loop(1, 5, merge_step, 0)
    local_out = pltpu.make_async_copy(ob.at[x], out_ref.at[:, lanes(x)], loc.at[0])
    local_out.start()

    g1, dd1 = g1s[...].reshape(512, LANES), d1s[...].reshape(512, LANES)
    gw1[0:4] = (a1[...] * g1).astype(BF16).reshape(4, LANES, LANES)
    gt1[0:4] = (a1[...] * dd1).reshape(4, LANES, LANES)
    g2 = paired(g2s, b1[...] * g1, 512)
    dd2 = paired(d2s, b1[...] * dd1, 512)
    gw1[4:6] = (own2 * g2).astype(BF16).reshape(2, LANES, LANES)
    gt1[4:6] = (own2 * dd2).reshape(2, LANES, LANES)
    g3 = paired(spm, rest2 * g2, 256)
    dd3 = paired(spn, rest2 * dd2, 256)
    gw1[6] = (a3 * g3).astype(BF16)
    gt1[6] = a3 * dd3
    pieces = []
    for share in shares_s:
        pieces.append(
            jnp.concatenate([(share * g3).astype(BF16), *split2(share * dd3)], axis=1)
        )
    pooled = mm(level_pool(), jnp.concatenate(pieces, axis=0))
    gw_s = pooled[:, :LANES].astype(BF16)
    gt_s = pooled[:, 128:256] + pooled[:, 256:384]

    grads_s = stack_grads(gw_s, gt_s)
    lift = pick(mm_nt(grads_s, far_vals), level)
    gs = (weights_s.astype(F32) * lift).astype(BF16)
    gs_blocks = blocks_of(gs, level)
    gk_far = mm_tn(gs_blocks, q_stack)
    gv_far = mm_tn(blocks_s, grads_s[:, :LANES])
    far_grads = jnp.concatenate([gk_far, gv_far], axis=1)
    g4s[...] = far_grads[:LANES].reshape(2, 64, 256)
    sb[...] = far_grads[LANES:].astype(BF16).reshape(32, 16, 256)

    back_b = []
    for m in range(1, 16):
        up = m.bit_length() - 1
        count = 8 >> up
        pw = flip(w, m, 4)
        theirs = 8 * up + (pw % 2**up) * count
        ours = 8 * up + (w % 2**up) * count
        copy = remote(
            sb.at[pl.ds(theirs, count)], rb.at[pl.ds(ours, count)],
            bb_send.at[m - 1], bb_recv.at[m - 1], place(x, y, pw),
        )
        copy.start()
        back_b.append(copy)

    gq_s = fold(mm(gs_blocks, far[:, :LANES]), LANES) * 0.125
    high, low = split2(gq_s)
    weighted_spread = spreads[0] * 0.5
    for index in range(1, 5):
        weighted_spread = weighted_spread + spreads[index] * 0.5 ** (index + 1)
    weighted_spread = weighted_spread.astype(BF16)
    run_q3 = mm(weighted_spread, high) + mm(weighted_spread, low)

    def unit_back(index, carry):
        unit = 6 - index
        other = unit + 1 - 2 * (unit % 2)
        gq, gkv = attend_back(qp[unit], kvp[other], w1[unit], gw1[unit], gt1[unit])
        gq1[unit] = gq
        gkv1[other] = gkv
        return carry

    lax.fori_loop(0, 7, unit_back, 0)

    run_q2 = gq1[4:6].reshape(256, LANES) + 0.5 * doubled(spm, gq1[6] + run_q3, 128)
    run_q1 = gq1[0:4].reshape(512, LANES) + 0.5 * doubled(spm, run_q2, 256)
    run_k2 = gkv1[4:6, :, :LANES].reshape(256, LANES)
    run_v2 = gkv1[4:6, :, LANES:].reshape(256, LANES)
    run_k1 = gkv1[0:4, :, :LANES].reshape(512, LANES) + 0.5 * doubled(spn, run_k2, 256)
    run_v1 = gkv1[0:4, :, LANES:].reshape(512, LANES) + 0.5 * doubled(spd, run_v2, 256)
    m1[...] = run_q1.reshape(4, LANES, LANES)
    n1[...] = run_k1.reshape(4, LANES, LANES)
    d1[...] = run_v1.reshape(4, LANES, LANES)

    def chunk_back(mask, carry):
        px = flip(x, mask, 2)
        gq, gkv = attend_back(qb[px], kvb[px], w0[px], gw0[px], gt0[px])
        oq[px] = (gq + 0.5 * doubled(spm, m1[px], 128)).astype(BF16)
        bk[px, :, :LANES] = (gkv[:, :LANES] + 0.5 * doubled(spn, n1[px], 128)).astype(BF16)
        bk[px, :, LANES:] = (gkv[:, LANES:] + 0.5 * doubled(spd, d1[px], 128)).astype(BF16)

        @pl.when(mask < 4)
        def _():
            output_copy(1, mask).start()
            output_copy(2, mask).start()

        return carry

    lax.fori_loop(1, 5, chunk_back, 0)
    local_q = pltpu.make_async_copy(oq.at[x], gq_ref.at[:, lanes(x)], loc.at[1])
    local_q.start()

    for copy in back_b:
        copy.wait_recv()
    shape = (LANES, LANES)
    row, col = iota(shape, 0), iota(shape, 1)
    gather = []
    for up in range(4):
        inside = jnp.bitwise_and(col, (LANES >> up) - 1)
        gather.append(jnp.where(shr(row, up) == inside, 0.5**up, 0.0))
    gather = jnp.concatenate(gather, axis=1).astype(BF16)
    run5 = mm(gather, rb[...].reshape(512, 256)).astype(BF16)
    t4[...] = mm(spread_matrix(LANES, 0.5), run5).reshape(4, 64, 256)
    m4s[y] = t4[y].astype(BF16).reshape(4, 16, 256)
    other_pair = 2 * (1 - y_pair)
    for half_index in range(2):
        slot = other_pair + half_index
        m4s[slot] = (t4[slot] + g4s[half_index]).astype(BF16).reshape(4, 16, 256)
    near = mm(spread_matrix(64, 0.5), t4[sib].astype(BF16)) + gkv1[7]
    m3s[...] = near.astype(BF16).reshape(4, 2, 16, 256)

    back_a = []
    for index, (mx, my) in enumerate(plane):
        px, py = flip(x, mx, 2), flip(y, my, 2)
        if my == 0:
            src, dst = m4s.at[py, pl.ds(px, 1)], cb.at[x, pl.ds(0, 1)]
        elif my == 1:
            src, dst = m3s.at[px], cb.at[x, pl.ds(1, 2)]
        else:
            src, dst = m4s.at[py, pl.ds(px, 1)], cb.at[x, pl.ds(3 + y_bit, 1)]
        copy = remote(src, dst, aa_send.at[index], aa_recv.at[index], place(px, py, w))
        copy.start()
        back_a.append(copy)
    cb[x, 0] = m4s[y, x]
    bkr[x] = bk[x]

    for mask in (1, 2, 3):
        for kind in range(3):
            output_copy(kind, mask).wait_recv()
    shape = (256, 80)
    token, unit = iota(shape, 0), iota(shape, 1)
    fine = (unit >= 16) & (unit < 48) & (shr(token, 3) == unit - 16)
    coarse = ((unit < 16) | (unit >= 48)) & (shr(token, 4) == jnp.bitwise_and(unit, 15))
    last = (jnp.where(fine, 0.125, 0.0) + jnp.where(coarse, 0.0625, 0.0)).astype(BF16)
    for copy in back_a:
        copy.wait_recv()
    for j in range(4):
        total = mm(last, cb[j].reshape(80, 256)) + bkr[j].astype(F32)
        gk_ref[:, j * LANES : (j + 1) * LANES] = total[:, :LANES].astype(BF16)
        gv_ref[:, j * LANES : (j + 1) * LANES] = total[:, LANES:].astype(BF16)

    local_out.wait()
    local_q.wait()
    for copies in (stage_a, stage_b, back_b, back_a):
        for copy in copies:
            copy.wait_send()
    for mask in (1, 2, 3):
        for copy in token_copies(mask):
            copy.wait_send()
        for kind in range(3):
            output_copy(kind, mask).wait_send()


def shards(query, key_in, value_in, grad_out):
    rows, width = query.shape
    whole = jax.ShapeDtypeStruct((rows, width), BF16)

    def f32(*shape):
        return pltpu.VMEM(shape, F32)

    def b16(*shape):
        return pltpu.VMEM(shape, BF16)

    dma = pltpu.SemaphoreType.DMA
    scratch = [
        b16(4, 256, 128), b16(4, 256, 256), b16(4, 256, 128),
        b16(4, 32, 256), b16(4, 16, 256),
        b16(4, 32, 256), b16(4, 32, 256), b16(4, 4, 16, 256),
        b16(8, 16, 256), b16(4, 16, 256), b16(2, 16, 256), b16(1, 16, 256),
        b16(32, 16, 256),
        b16(7, 128, 128), b16(8, 128, 256),
        b16(4, 512, 256), b16(7, 256, 128),
        f32(4, 256, 128), f32(4, 256, 128), f32(4, 256, 128),
        f32(7, 128, 128), f32(7, 128, 128), f32(7, 128, 128),
        f32(512, 128), f32(512, 128),
        f32(4, 128, 128), f32(4, 128, 128), f32(4, 128, 128),
        b16(4, 256, 128), f32(4, 256, 128), b16(7, 128, 128), f32(7, 128, 128),
        f32(512, 128), f32(512, 128), f32(512, 128),
        f32(4, 128, 128), f32(4, 128, 128), f32(512, 128), f32(512, 128),
        b16(4, 256, 128), b16(4, 256, 128), b16(4, 256, 256), b16(4, 256, 256),
        f32(7, 128, 128), f32(8, 128, 256), f32(8, 128),
        b16(32, 16, 256), b16(32, 16, 256),
        f32(4, 64, 256), b16(4, 2, 16, 256), b16(4, 4, 16, 256),
        b16(4, 5, 16, 256), f32(2, 64, 256),
        dma((4, 3)), dma((4, 3)), dma((15,)), dma((15,)), dma((15,)), dma((15,)),
        dma((15,)), dma((15,)), dma((15,)), dma((15,)), dma((3, 3)), dma((3, 3)), dma((2,)),
    ]
    vmem = pl.BlockSpec(memory_space=pltpu.VMEM)
    anywhere = pl.BlockSpec(memory_space=pl.ANY)
    return pl.pallas_call(
        kernel,
        out_shape=(whole, whole, whole, whole),
        in_specs=[vmem] * 4,
        out_specs=(anywhere, anywhere, vmem, vmem),
        scratch_shapes=scratch,
        compiler_params=pltpu.CompilerParams(
            collective_id=0, has_side_effects=True, vmem_limit_bytes=40 * 2**20
        ),
    )(query, key_in, value_in, grad_out)


def solution(mesh):
    spec = P(("grp", "seq"), None)
    return jax.shard_map(
        shards, mesh=mesh, in_specs=(spec,) * 4, out_specs=(spec,) * 4, check_vma=False
    )
```

```python
import functools

import jax
import jax.numpy as jnp
from jax import lax
from jax.experimental import pallas as pl
from jax.experimental.pallas import tpu as pltpu
from jax.sharding import PartitionSpec as P

MESH = pl.DeviceIdType.MESH
F32 = jnp.float32
BF16 = jnp.bfloat16
LANES = 128
NT = (((1,), (1,)), ((), ()))
TN = (((0,), (0,)), ((), ()))


def flip(value, mask, bits):
    out = 0
    for bit in range(bits):
        own = (value // 2**bit) % 2
        if isinstance(mask, int):
            out = out + 2**bit * (1 - own if (mask >> bit) & 1 else own)
        else:
            out = out + 2**bit * ((own + (mask // 2**bit) % 2) % 2)
    return out


def iota(shape, dim):
    return lax.broadcasted_iota(jnp.int32, shape, dim)


def shr(value, amount):
    return jnp.right_shift(value, amount)


def mm(a, b):
    return jnp.dot(a, b, preferred_element_type=F32)


def mm_nt(a, b):
    return lax.dot_general(a, b, NT, preferred_element_type=F32)


def mm_tn(a, b):
    return lax.dot_general(a, b, TN, preferred_element_type=F32)


def pool_matrix(rows, weight=0.5):
    shape = (rows // 2, rows)
    return jnp.where(shr(iota(shape, 1), 1) == iota(shape, 0), weight, 0.0).astype(BF16)


def spread_matrix(rows, weight):
    shape = (2 * rows, rows)
    return jnp.where(shr(iota(shape, 0), 1) == iota(shape, 1), weight, 0.0).astype(BF16)


def coarsen(values):
    return mm(pool_matrix(values.shape[0]), values).astype(BF16)


def lane_low():
    return iota((1, LANES), 1) < 64


def head_masks(weight):
    low = lane_low()
    return (
        jnp.where(low, weight, 0.0).astype(BF16),
        jnp.where(low, 0.0, weight).astype(BF16),
    )


def with_ones(vals):
    return jnp.concatenate([vals, jnp.ones_like(vals)], axis=1)


def fold(stacked, rows):
    return jnp.where(lane_low(), stacked[:rows], stacked[rows:])


def split2(values):
    high = values.astype(BF16)
    return high, (values - high.astype(F32)).astype(BF16)


def stack_heads(q):
    low, high = head_masks(0.125)
    return jnp.concatenate([q * low, q * high], axis=0)


def soft_weights(scores):
    peak = jnp.max(scores, axis=1, keepdims=True).astype(BF16).astype(F32)
    return jnp.exp(scores - peak).astype(BF16), peak


def attend(q, kv):
    rows = q.shape[0]
    scores = mm_nt(stack_heads(q), kv[:, :LANES])
    weights, peak = soft_weights(scores)
    both = mm(weights, with_ones(kv[:, LANES:]))
    weighted = fold(both[:, :LANES], rows)
    total = fold(both[:, LANES:], rows)
    wide = jnp.broadcast_to(peak, (2 * rows, LANES))
    return weights, fold(wide, rows), weighted, total


def stack_grads(gw, gt):
    low, high = head_masks(1.0)
    lane = iota((1, LANES), 1)
    first = jnp.where((lane == 0) | (lane == 64), 1.0, 0.0).astype(BF16)
    second = jnp.where((lane == 1) | (lane == 65), 1.0, 0.0).astype(BF16)
    gt_high, gt_low = split2(gt)
    extra = gt_high * first + gt_low * second
    return jnp.concatenate(
        [
            jnp.concatenate([gw * low, extra * low], axis=1),
            jnp.concatenate([gw * high, extra * high], axis=1),
        ],
        axis=0,
    )


def attend_back(q, kv, weights, gw, gt):
    rows = q.shape[0]
    stacked = stack_grads(gw, gt)
    lift = mm_nt(stacked, with_ones(kv[:, LANES:]))
    gs = (weights.astype(F32) * lift).astype(BF16)
    gv = mm_tn(weights, stacked[:, :LANES])
    gk = mm_tn(gs, stack_heads(q))
    gq = fold(mm(gs, kv[:, :LANES]), rows) * 0.125
    return gq, jnp.concatenate([gk, gv], axis=1)


OFFS = (0, 64, 96, 112, 120)


def row_level(row):
    level = jnp.zeros_like(row)
    for edge in OFFS[1:]:
        level = level + jnp.where(row >= edge, 1, 0)
    return level


def pick(full, level, width=LANES):
    out = jnp.where(level == 0, full[:, :width], 0.0)
    for index in range(1, 5):
        out = jnp.where(level == index, full[:, index * width : (index + 1) * width], out)
    return out


def blocks_of(values, level):
    zero = jnp.zeros_like(values)
    return jnp.concatenate([jnp.where(level == i, values, zero) for i in range(5)], axis=1)


def level_spread():
    parts = []
    shape = (LANES, LANES)
    row, col = iota(shape, 0), iota(shape, 1)
    for index, start in enumerate(OFFS):
        parts.append(jnp.where(col == start + shr(row, index + 1), 1.0, 0.0))
    return parts


def level_pool():
    parts = []
    shape = (LANES, LANES)
    row, col = iota(shape, 0), iota(shape, 1)
    for index, start in enumerate(OFFS):
        parts.append(jnp.where(row == start + shr(col, index + 1), 1.0, 0.0))
    return jnp.concatenate(parts, axis=1).astype(BF16)


def kernel(
    q_hbm, k_hbm, v_hbm, g_hbm, out_ref, gq_ref, cb, bkr,
    q_ref, k_ref, v_ref, g_ref, qb, kvb, gb, l3, l4, kv3sib, r4, own5, own6, own7, own8, rf,
    qp, kvp, w0, w1, w0w, w0p, w0t, w1w, w1p, w1t,
    m1, n1, d1, gw0, gt0, gw1, gt1, sp, g1s, d1s,
    ob, oq, bk, gq1, gkv1, sb, rb, t4, m3s, m4s, g4s,
    p_send, p_recv, a_send, a_recv, c_send, c_recv, b_send, b_recv, bb_send, bb_recv,
    aa_send, aa_recv, o_send, o_recv, loc,
):
    grp, seq = lax.axis_index("grp"), lax.axis_index("seq")
    x, y = seq % 4, (seq // 4) % 4
    w = grp * 2 + seq // 16
    y_pair, y_bit = y // 2, y % 2
    sib = flip(y, 1, 2)

    def place(px, py, pw):
        return (pw // 2, (pw % 2) * 16 + py * 4 + px)

    def remote(src, dst, send, recv, device):
        return pltpu.make_async_remote_copy(
            src_ref=src, dst_ref=dst, send_sem=send, recv_sem=recv,
            device_id=device, device_id_type=MESH,
        )

    plane = [(mx, my) for my in (1, 2, 3, 0) for mx in range(4) if (mx, my) != (0, 0)]

    barrier = pltpu.get_barrier_semaphore()
    for mx, my in plane:
        pl.semaphore_signal(
            barrier, inc=1, device_id=place(flip(x, mx, 2), flip(y, my, 2), w), device_id_type=MESH
        )
    for m in range(1, 16):
        pl.semaphore_signal(
            barrier, inc=1, device_id=place(x, y, flip(w, m, 4)), device_id_type=MESH
        )

    loads = []
    for index, (src, dst) in enumerate(
        ((k_hbm, k_ref), (v_hbm, v_ref), (q_hbm, q_ref), (g_hbm, g_ref))
    ):
        copy = pltpu.make_async_copy(src, dst, loc.at[index])
        copy.start()
        loads.append(copy)

    for part, ref in ((0, k_ref), (1, v_ref)):
        loads[part].wait()
        rows = coarsen(coarsen(coarsen(ref[...])))
        upper = coarsen(rows)
        for j in range(4):
            l3[j, :, part * LANES : (part + 1) * LANES] = rows[:, j * LANES : (j + 1) * LANES]
            l4[j, :, part * LANES : (part + 1) * LANES] = upper[:, j * LANES : (j + 1) * LANES]

    loads[2].wait()
    loads[3].wait()
    pl.semaphore_wait(barrier, 30)

    stage_a = []
    for index, (mx, my) in enumerate(plane):
        px, py = flip(x, mx, 2), flip(y, my, 2)
        copy = remote(
            l4.at[px], r4.at[y, x], a_send.at[index], a_recv.at[index], place(px, py, w)
        )
        copy.start()
        stage_a.append(copy)

    def lanes(index):
        return pl.ds(pl.multiple_of(index * LANES, LANES), LANES)

    def token_copies(mask):
        px = flip(x, mask, 2)
        device = place(px, y, w)
        pairs = (
            (k_ref, kvb.at[x, :, pl.ds(0, LANES)]),
            (v_ref, kvb.at[x, :, pl.ds(LANES, LANES)]),
            (q_ref, qb.at[x]),
            (g_ref, gb.at[x]),
        )
        return [
            remote(
                ref.at[:, lanes(px)], dst, p_send.at[i, mask - 1], p_recv.at[i, mask - 1], device
            )
            for i, (ref, dst) in enumerate(pairs)
        ]

    moves = {mask: token_copies(mask) for mask in (1, 2, 3)}
    for i in range(3):
        moves[1][i].start()
        moves[3][i].start()
    stage_c = []
    for mx in range(4):
        px = flip(x, mx, 2)
        copy = remote(l3.at[px], kv3sib.at[x], c_send.at[mx], c_recv.at[mx], place(px, sib, w))
        copy.start()
        stage_c.append(copy)
    for i in range(3):
        moves[2][i].start()
    for mask in (1, 3, 2):
        moves[mask][3].start()

    kvb[x, :, :LANES] = k_ref[:, lanes(x)]
    kvb[x, :, LANES:] = v_ref[:, lanes(x)]
    qb[x] = q_ref[:, lanes(x)]
    gb[x] = g_ref[:, lanes(x)]
    r4[y, x] = l4[x]

    def chunk_forward(slot):
        q, kv = qb[slot], kvb[slot]
        weights, peak, weighted, total = attend(q, kv)
        w0[slot] = weights
        w0p[slot], w0w[slot], w0t[slot] = peak, weighted, total
        qp[slot] = coarsen(q)
        kvp[slot] = coarsen(kv)

    chunk_forward(x)

    for copy in stage_a:
        copy.wait_recv()
    half = pool_matrix(LANES)
    rows5 = coarsen(r4[...].reshape(256, 256))
    rows6 = coarsen(rows5)
    rows7 = coarsen(rows6)
    rows8 = coarsen(rows7)
    own5[...] = rows5.reshape(8, 16, 256)
    own6[...] = rows6.reshape(4, 16, 256)
    own7[...] = rows7.reshape(2, 16, 256)
    own8[...] = rows8.reshape(1, 16, 256)

    stage_b = []
    owns = (own5, own6, own7, own8)
    for m in range(1, 16):
        up = m.bit_length() - 1
        count = 8 >> up
        start = 8 * up + (w % 2**up) * count
        copy = remote(
            owns[up], rf.at[pl.ds(start, count)], b_send.at[m - 1], b_recv.at[m - 1],
            place(x, y, flip(w, m, 4)),
        )
        copy.start()
        stage_b.append(copy)

    def unit_forward(unit, other):
        weights, peak, weighted, total = attend(qp[unit], kvp[other])
        w1[unit] = weights
        w1p[unit], w1w[unit], w1t[unit] = peak, weighted, total

    for mask in (1, 3, 2):
        for copy in moves[mask][:3]:
            copy.wait_recv()
        chunk_forward(flip(x, mask, 2))
        if mask == 1:
            unit_forward(x, flip(x, 1, 2))
            unit_forward(flip(x, 1, 2), x)
    unit_forward(flip(x, 3, 2), flip(x, 2, 2))
    unit_forward(flip(x, 2, 2), flip(x, 3, 2))
    for copy in stage_c:
        copy.wait_recv()
    kvp[7] = kv3sib[...].reshape(LANES, 256)
    qp[4] = coarsen(qp[0:2].reshape(256, LANES))
    qp[5] = coarsen(qp[2:4].reshape(256, LANES))
    kvp[4] = coarsen(kvp[0:2].reshape(256, 256))
    kvp[5] = coarsen(kvp[2:4].reshape(256, 256))
    qp[6] = coarsen(qp[4:6].reshape(256, LANES))
    for unit in (4, 5, 6):
        unit_forward(unit, unit ^ 1)

    qs = mm(half, qp[6])
    qs = jnp.concatenate([qs, jnp.zeros((64, LANES), F32)], axis=0)
    shape = (LANES, LANES)
    row, col = iota(shape, 0), iota(shape, 1)
    down = jnp.where((row >= 64) & (shr(col, 1) == row - 64), 0.5, 0.0).astype(BF16)
    qs = qs.astype(BF16)
    upper_rows = iota((LANES, 1), 0) >= 64
    for _ in range(4):
        qs = jnp.where(upper_rows, mm(down, qs), qs.astype(F32)).astype(BF16)
    level = row_level(jnp.bitwise_and(iota((256, 1), 0), 127))

    for copy in stage_b:
        copy.wait_recv()
    far4 = r4[pl.ds(2 * (1 - y_pair), 2)].reshape(LANES, 256)
    far = jnp.concatenate([far4, rf[...].reshape(512, 256)], axis=0)
    far_vals = with_ones(far[:, LANES:])
    q_stack = stack_heads(qs)
    weights_s, peak_s = soft_weights(pick(mm_nt(q_stack, far[:, :LANES]), level))
    blocks_s = blocks_of(weights_s, level)
    both = mm(blocks_s, far_vals)
    weighted_s = fold(both[:, :LANES], LANES)
    total_s = fold(both[:, LANES:], LANES)
    peak_s = fold(jnp.broadcast_to(peak_s, (256, LANES)), LANES)

    spreads = level_spread()
    stats = jnp.concatenate(
        [peak_s.astype(BF16), *split2(weighted_s), *split2(total_s)], axis=1
    )
    taken = [mm(part.astype(BF16), stats) for part in spreads]
    m3 = w1p[6]
    for t in taken:
        m3 = jnp.maximum(m3, t[:, :LANES])
    a3 = jnp.exp(w1p[6] - m3)
    n3, d3 = a3 * w1w[6], a3 * w1t[6]
    shares_s = []
    for index, t in enumerate(taken):
        share = 2.0 ** (index + 1) * jnp.exp(t[:, :LANES] - m3)
        n3 = n3 + share * (t[:, 128:256] + t[:, 256:384])
        d3 = d3 + share * (t[:, 384:512] + t[:, 512:640])
        shares_s.append(share)

    used = [0]

    def fresh():
        used[0] += 1
        return sp.at[used[0] - 1]

    def doubled(values):
        count, ref = values.shape[0], fresh()
        ref[pl.ds(0, count, 2), :] = values
        ref[pl.ds(1, count, 2), :] = values
        return ref[0 : 2 * count, :]

    def paired(values):
        count, ref = values.shape[0], fresh()
        ref[0:count, :] = values
        return ref[pl.ds(0, count // 2, 2), :] + ref[pl.ds(1, count // 2, 2), :]

    def merge(peak, weighted, total, m, n, d):
        crest = jnp.maximum(peak, m)
        own = jnp.exp(peak - crest)
        rest = 2.0 * jnp.exp(m - crest)
        return crest, own * weighted + rest * n, own * total + rest * d, own, rest

    m2, n2, d2, own2, rest2 = merge(
        w1p[4:6].reshape(256, LANES), w1w[4:6].reshape(256, LANES), w1t[4:6].reshape(256, LANES),
        doubled(m3), doubled(n3), doubled(d3),
    )
    crest1, n1v, d1v, own1, rest1 = merge(
        w1p[0:4].reshape(512, LANES), w1w[0:4].reshape(512, LANES), w1t[0:4].reshape(512, LANES),
        doubled(m2), doubled(n2), doubled(d2),
    )
    m1[...] = crest1.reshape(4, LANES, LANES)
    n1[...] = n1v.reshape(4, LANES, LANES)
    d1[...] = d1v.reshape(4, LANES, LANES)

    same = jnp.where(shr(iota(shape, 0), 6) == shr(iota(shape, 1), 6), 1.0, 0.0).astype(BF16)
    head_sum = jnp.concatenate([same, same], axis=0)

    def output_copy(kind, mask):
        px = flip(x, mask, 2)
        if kind == 0:
            src, dst = ob.at[px], out_ref.at[:, lanes(x)]
        elif kind == 1:
            src, dst = oq.at[px], gq_ref.at[:, lanes(x)]
        else:
            src, dst = bk.at[px], bkr.at[x]
        return remote(
            src, dst, o_send.at[kind, mask - 1], o_recv.at[kind, mask - 1], place(px, y, w)
        )

    for mask in (1, 3, 2):
        moves[mask][3].wait_recv()
    for mask in (1, 3, 2, 0):
        px = flip(x, mask, 2)
        crest, numer, denom, own, rest = merge(
            w0p[px], w0w[px], w0t[px], doubled(m1[px]), doubled(n1[px]), doubled(d1[px])
        )
        inverse = 1.0 / denom
        ratio = numer * inverse
        up = gb[px].astype(F32)
        high, low = split2(up * ratio)
        drift = -mm(jnp.concatenate([high, low], axis=1), head_sum) * inverse
        scaled = up * inverse
        if mask:
            ob[px] = ratio.astype(BF16)
        else:
            out_ref[:, lanes(x)] = ratio.astype(BF16)
        gw0[px] = (own * scaled).astype(BF16)
        gt0[px] = own * drift
        g1s[px] = paired(rest * scaled)
        d1s[px] = paired(rest * drift)
    outs = {(kind, mask): output_copy(kind, mask) for kind in range(3) for mask in (1, 3, 2)}
    for mask in (1, 3, 2):
        outs[0, mask].start()

    g1, dd1 = g1s[...].reshape(512, LANES), d1s[...].reshape(512, LANES)
    gw1[0:4] = (own1 * g1).astype(BF16).reshape(4, LANES, LANES)
    gt1[0:4] = (own1 * dd1).reshape(4, LANES, LANES)
    g2 = paired(rest1 * g1)
    dd2 = paired(rest1 * dd1)
    gw1[4:6] = (own2 * g2).astype(BF16).reshape(2, LANES, LANES)
    gt1[4:6] = (own2 * dd2).reshape(2, LANES, LANES)
    g3 = paired(rest2 * g2)
    dd3 = paired(rest2 * dd2)
    gw1[6] = (a3 * g3).astype(BF16)
    gt1[6] = a3 * dd3
    pieces = []
    for share in shares_s:
        pieces.append(
            jnp.concatenate([(share * g3).astype(BF16), *split2(share * dd3)], axis=1)
        )
    pooled = mm(level_pool(), jnp.concatenate(pieces, axis=0))
    gw_s = pooled[:, :LANES].astype(BF16)
    gt_s = pooled[:, 128:256] + pooled[:, 256:384]

    grads_s = stack_grads(gw_s, gt_s)
    lift = pick(mm_nt(grads_s, far_vals), level)
    gs = (weights_s.astype(F32) * lift).astype(BF16)
    gs_blocks = blocks_of(gs, level)
    gk_far = mm_tn(gs_blocks, q_stack)
    gv_far = mm_tn(blocks_s, grads_s[:, :LANES])
    far_grads = jnp.concatenate([gk_far, gv_far], axis=1)
    g4s[...] = far_grads[:LANES].reshape(2, 64, 256)
    sb[...] = far_grads[LANES:].astype(BF16).reshape(32, 16, 256)

    back_b = []
    for m in range(1, 16):
        up = m.bit_length() - 1
        count = 8 >> up
        pw = flip(w, m, 4)
        theirs = 8 * up + (pw % 2**up) * count
        ours = 8 * up + (w % 2**up) * count
        copy = remote(
            sb.at[pl.ds(theirs, count)], rb.at[pl.ds(ours, count)],
            bb_send.at[m - 1], bb_recv.at[m - 1], place(x, y, pw),
        )
        copy.start()
        back_b.append(copy)

    gq_s = fold(mm(gs_blocks, far[:, :LANES]), LANES) * 0.125
    high, low = split2(gq_s)
    weighted_spread = spreads[0] * 0.5
    for index in range(1, 5):
        weighted_spread = weighted_spread + spreads[index] * 0.5 ** (index + 1)
    weighted_spread = weighted_spread.astype(BF16)
    run_q3 = mm(weighted_spread, high) + mm(weighted_spread, low)

    for unit in range(6, -1, -1):
        gq1[unit], gkv1[unit ^ 1] = attend_back(
            qp[unit], kvp[unit ^ 1], w1[unit], gw1[unit], gt1[unit]
        )

    run_q2 = gq1[4:6].reshape(256, LANES) + 0.5 * doubled(gq1[6] + run_q3)
    run_q1 = gq1[0:4].reshape(512, LANES) + 0.5 * doubled(run_q2)
    run_k2 = gkv1[4:6, :, :LANES].reshape(256, LANES)
    run_v2 = gkv1[4:6, :, LANES:].reshape(256, LANES)
    run_k1 = gkv1[0:4, :, :LANES].reshape(512, LANES) + 0.5 * doubled(run_k2)
    run_v1 = gkv1[0:4, :, LANES:].reshape(512, LANES) + 0.5 * doubled(run_v2)
    m1[...] = run_q1.reshape(4, LANES, LANES)
    n1[...] = run_k1.reshape(4, LANES, LANES)
    d1[...] = run_v1.reshape(4, LANES, LANES)

    for mask in (1, 3, 2, 0):
        px = flip(x, mask, 2)
        gq, gkv = attend_back(qb[px], kvb[px], w0[px], gw0[px], gt0[px])
        gq = (gq + 0.5 * doubled(m1[px])).astype(BF16)
        gk = (gkv[:, :LANES] + 0.5 * doubled(n1[px])).astype(BF16)
        gv = (gkv[:, LANES:] + 0.5 * doubled(d1[px])).astype(BF16)
        if mask:
            oq[px] = gq
            bk[px, :, :LANES] = gk
            bk[px, :, LANES:] = gv
            outs[1, mask].start()
            outs[2, mask].start()
        else:
            gq_ref[:, lanes(x)] = gq
            bkr[x, :, :LANES] = gk
            bkr[x, :, LANES:] = gv

    for copy in back_b:
        copy.wait_recv()
    shape = (LANES, LANES)
    row, col = iota(shape, 0), iota(shape, 1)
    gather = []
    for up in range(4):
        inside = jnp.bitwise_and(col, (LANES >> up) - 1)
        gather.append(jnp.where(shr(row, up) == inside, 0.5**up, 0.0))
    gather = jnp.concatenate(gather, axis=1).astype(BF16)
    run5 = mm(gather, rb[...].reshape(512, 256)).astype(BF16)
    t4[...] = mm(spread_matrix(LANES, 0.5), run5).reshape(4, 64, 256)
    m4s[y] = t4[y].astype(BF16).reshape(4, 16, 256)
    other_pair = 2 * (1 - y_pair)
    for half_index in range(2):
        slot = other_pair + half_index
        m4s[slot] = (t4[slot] + g4s[half_index]).astype(BF16).reshape(4, 16, 256)
    near = mm(spread_matrix(64, 0.5), t4[sib].astype(BF16)) + gkv1[7]
    m3s[...] = near.astype(BF16).reshape(4, 2, 16, 256)

    back_a = []
    for index, (mx, my) in enumerate(plane):
        px, py = flip(x, mx, 2), flip(y, my, 2)
        if my == 0:
            src, dst = m4s.at[py, pl.ds(px, 1)], cb.at[x, pl.ds(0, 1)]
        elif my == 1:
            src, dst = m3s.at[px], cb.at[x, pl.ds(1, 2)]
        else:
            src, dst = m4s.at[py, pl.ds(px, 1)], cb.at[x, pl.ds(3 + y_bit, 1)]
        copy = remote(src, dst, aa_send.at[index], aa_recv.at[index], place(px, py, w))
        copy.start()
        back_a.append(copy)
    cb[x, 0] = m4s[y, x]

    for copy in back_a:
        copy.wait_recv()
    for copy in outs.values():
        copy.wait_recv()
    for copies in (stage_a, stage_b, stage_c, back_b, back_a, outs.values(), *moves.values()):
        for copy in copies:
            copy.wait_send()


def finish(out_v, gq_v, cb, bkr, out_ref, gq_ref, gk_ref, gv_ref, gk_v, gv_v, sems):
    first = pltpu.make_async_copy(out_v, out_ref, sems.at[0])
    second = pltpu.make_async_copy(gq_v, gq_ref, sems.at[1])
    first.start()
    second.start()
    shape = (256, 80)
    token, unit = iota(shape, 0), iota(shape, 1)
    fine = (unit >= 16) & (unit < 48) & (shr(token, 3) == unit - 16)
    coarse = ((unit < 16) | (unit >= 48)) & (shr(token, 4) == jnp.bitwise_and(unit, 15))
    last = (jnp.where(fine, 0.125, 0.0) + jnp.where(coarse, 0.0625, 0.0)).astype(BF16)
    for j in range(4):
        total = mm(last, cb[j].reshape(80, 256)) + bkr[j].astype(F32)
        gk_v[:, j * LANES : (j + 1) * LANES] = total[:, :LANES].astype(BF16)
        gv_v[:, j * LANES : (j + 1) * LANES] = total[:, LANES:].astype(BF16)
    third = pltpu.make_async_copy(gk_v, gk_ref, sems.at[2])
    fourth = pltpu.make_async_copy(gv_v, gv_ref, sems.at[3])
    third.start()
    fourth.start()
    for copy in (first, second, third, fourth):
        copy.wait()


def shards(query, key_in, value_in, grad_out):
    rows, width = query.shape
    whole = jax.ShapeDtypeStruct((rows, width), BF16)

    def f32(*shape):
        return pltpu.VMEM(shape, F32)

    def b16(*shape):
        return pltpu.VMEM(shape, BF16)

    dma = pltpu.SemaphoreType.DMA
    scratch = [
        b16(256, 512), b16(256, 512), b16(256, 512), b16(256, 512),
        b16(4, 256, 128), b16(4, 256, 256), b16(4, 256, 128),
        b16(4, 32, 256), b16(4, 16, 256), b16(4, 32, 256), b16(4, 4, 16, 256),
        b16(8, 16, 256), b16(4, 16, 256), b16(2, 16, 256), b16(1, 16, 256),
        b16(32, 16, 256),
        b16(7, 128, 128), b16(8, 128, 256),
        b16(4, 512, 256), b16(7, 256, 128),
        f32(4, 256, 128), f32(4, 256, 128), f32(4, 256, 128),
        f32(7, 128, 128), f32(7, 128, 128), f32(7, 128, 128),
        f32(4, 128, 128), f32(4, 128, 128), f32(4, 128, 128),
        b16(4, 256, 128), f32(4, 256, 128), b16(7, 128, 128), f32(7, 128, 128),
        f32(48, 512, 128), f32(4, 128, 128), f32(4, 128, 128),
        b16(4, 256, 128), b16(4, 256, 128), b16(4, 256, 256),
        f32(7, 128, 128), f32(8, 128, 256),
        b16(32, 16, 256), b16(32, 16, 256),
        f32(4, 64, 256), b16(4, 2, 16, 256), b16(4, 4, 16, 256), f32(2, 64, 256),
        dma((4, 3)), dma((4, 3)), dma((15,)), dma((15,)), dma((4,)), dma((4,)),
        dma((15,)), dma((15,)), dma((15,)), dma((15,)), dma((15,)), dma((15,)),
        dma((3, 3)), dma((3, 3)), dma((4,)),
    ]
    vmem = pl.BlockSpec(memory_space=pltpu.VMEM)
    hbm = pl.BlockSpec(memory_space=pltpu.HBM)
    parts = pl.pallas_call(
        kernel,
        out_shape=(
            whole, whole,
            jax.ShapeDtypeStruct((4, 5, 16, 256), BF16), jax.ShapeDtypeStruct((4, 256, 256), BF16),
        ),
        in_specs=[hbm] * 4,
        out_specs=(vmem,) * 4,
        scratch_shapes=scratch,
        compiler_params=pltpu.CompilerParams(
            collective_id=0, has_side_effects=True, vmem_limit_bytes=40 * 2**20
        ),
    )(query, key_in, value_in, grad_out)
    return pl.pallas_call(
        finish,
        out_shape=(whole,) * 4,
        in_specs=[vmem] * 4,
        out_specs=(hbm,) * 4,
        scratch_shapes=[b16(256, 512), b16(256, 512), dma((4,))],
        compiler_params=pltpu.CompilerParams(vmem_limit_bytes=8 * 2**20),
    )(*parts)


def solution(mesh):
    spec = P(("grp", "seq"), None)
    return jax.shard_map(
        shards, mesh=mesh, in_specs=(spec,) * 4, out_specs=(spec,) * 4, check_vma=False
    )
```

```python
import functools

import jax
import jax.numpy as jnp
from jax import lax
from jax.experimental import pallas as pl
from jax.experimental.pallas import tpu as pltpu
from jax.sharding import PartitionSpec as P

MESH = pl.DeviceIdType.MESH
F32 = jnp.float32
BF16 = jnp.bfloat16
LANES = 128
NT = (((1,), (1,)), ((), ()))
TN = (((0,), (0,)), ((), ()))


def flip(value, mask, bits):
    out = 0
    for bit in range(bits):
        own = (value // 2**bit) % 2
        if isinstance(mask, int):
            out = out + 2**bit * (1 - own if (mask >> bit) & 1 else own)
        else:
            out = out + 2**bit * ((own + (mask // 2**bit) % 2) % 2)
    return out


def iota(shape, dim):
    return lax.broadcasted_iota(jnp.int32, shape, dim)


def shr(value, amount):
    return jnp.right_shift(value, amount)


def mm(a, b):
    return jnp.dot(a, b, preferred_element_type=F32)


def mm_nt(a, b):
    return lax.dot_general(a, b, NT, preferred_element_type=F32)


def mm_tn(a, b):
    return lax.dot_general(a, b, TN, preferred_element_type=F32)


def pool_matrix(rows, weight=0.5):
    shape = (rows // 2, rows)
    return jnp.where(shr(iota(shape, 1), 1) == iota(shape, 0), weight, 0.0).astype(BF16)


def spread_matrix(rows, weight):
    shape = (2 * rows, rows)
    return jnp.where(shr(iota(shape, 0), 1) == iota(shape, 1), weight, 0.0).astype(BF16)


def coarsen(values):
    return mm(pool_matrix(values.shape[0]), values).astype(BF16)


def lane_low():
    return iota((1, LANES), 1) < 64


def head_masks(weight):
    low = lane_low()
    return (
        jnp.where(low, weight, 0.0).astype(BF16),
        jnp.where(low, 0.0, weight).astype(BF16),
    )


def with_ones(vals):
    return jnp.concatenate([vals, jnp.ones_like(vals)], axis=1)


def fold(stacked, rows):
    return jnp.where(lane_low(), stacked[:rows], stacked[rows:])


def split2(values):
    high = values.astype(BF16)
    return high, (values - high.astype(F32)).astype(BF16)


def stack_heads(q):
    low, high = head_masks(0.125)
    return jnp.concatenate([q * low, q * high], axis=0)


def soft_weights(scores):
    peak = jnp.max(scores, axis=1, keepdims=True).astype(BF16).astype(F32)
    return jnp.exp(scores - peak).astype(BF16), peak


def attend(q, kv):
    rows = q.shape[0]
    scores = mm_nt(stack_heads(q), kv[:, :LANES])
    weights, peak = soft_weights(scores)
    both = mm(weights, with_ones(kv[:, LANES:]))
    weighted = fold(both[:, :LANES], rows)
    total = fold(both[:, LANES:], rows)
    wide = jnp.broadcast_to(peak, (2 * rows, LANES))
    return weights, fold(wide, rows), weighted, total


def stack_grads(gw, gt):
    low, high = head_masks(1.0)
    lane = iota((1, LANES), 1)
    first = jnp.where((lane == 0) | (lane == 64), 1.0, 0.0).astype(BF16)
    second = jnp.where((lane == 1) | (lane == 65), 1.0, 0.0).astype(BF16)
    gt_high, gt_low = split2(gt)
    extra = gt_high * first + gt_low * second
    return jnp.concatenate(
        [
            jnp.concatenate([gw * low, extra * low], axis=1),
            jnp.concatenate([gw * high, extra * high], axis=1),
        ],
        axis=0,
    )


def attend_back(q, kv, weights, gw, gt):
    rows = q.shape[0]
    stacked = stack_grads(gw, gt)
    lift = mm_nt(stacked, with_ones(kv[:, LANES:]))
    gs = (weights.astype(F32) * lift).astype(BF16)
    gv = mm_tn(weights, stacked[:, :LANES])
    gk = mm_tn(gs, stack_heads(q))
    gq = fold(mm(gs, kv[:, :LANES]), rows) * 0.125
    return gq, jnp.concatenate([gk, gv], axis=1)


OFFS = (0, 64, 96, 112, 120)


def row_level(row):
    level = jnp.zeros_like(row)
    for edge in OFFS[1:]:
        level = level + jnp.where(row >= edge, 1, 0)
    return level


def pick(full, level, width=LANES):
    out = jnp.where(level == 0, full[:, :width], 0.0)
    for index in range(1, 5):
        out = jnp.where(level == index, full[:, index * width : (index + 1) * width], out)
    return out


def blocks_of(values, level):
    zero = jnp.zeros_like(values)
    return jnp.concatenate([jnp.where(level == i, values, zero) for i in range(5)], axis=1)


def level_spread():
    parts = []
    shape = (LANES, LANES)
    row, col = iota(shape, 0), iota(shape, 1)
    for index, start in enumerate(OFFS):
        parts.append(jnp.where(col == start + shr(row, index + 1), 1.0, 0.0))
    return parts


def level_pool():
    parts = []
    shape = (LANES, LANES)
    row, col = iota(shape, 0), iota(shape, 1)
    for index, start in enumerate(OFFS):
        parts.append(jnp.where(row == start + shr(col, index + 1), 1.0, 0.0))
    return jnp.concatenate(parts, axis=1).astype(BF16)


def kernel(
    q_hbm, k_hbm, v_hbm, g_hbm, out_ref, gq_ref, cb, bkr,
    k_ref, v_ref, qb, kvb, gb, l4, own3, kv3sib, r4, own5, own6, own7, own8, rf,
    qp, kvp, w0, w1, w0w, w0p, w0t, w1w, w1p, w1t,
    m1, n1, d1, gw0, gt0, gw1, gt1, sp, g1s, d1s,
    ob, oq, bk, gq1, gkv1, sb, rb, s3, s4, s5, e3, e4, e5, cs, ratios, inverses,
    p_send, p_recv, a_send, a_recv, c_send, c_recv, b_send, b_recv, bb_send, bb_recv,
    ey_send, ey_recv, e5_send, e5_recv, cx_send, cx_recv, o_send, o_recv, loc,
):
    grp, seq = lax.axis_index("grp"), lax.axis_index("seq")
    x, y = seq % 4, (seq // 4) % 4
    w = grp * 2 + seq // 16
    y_pair, y_bit = y // 2, y % 2
    sib = flip(y, 1, 2)

    def place(px, py, pw):
        return (pw // 2, (pw % 2) * 16 + py * 4 + px)

    def remote(src, dst, send, recv, device):
        return pltpu.make_async_remote_copy(
            src_ref=src, dst_ref=dst, send_sem=send, recv_sem=recv,
            device_id=device, device_id_type=MESH,
        )

    barrier = pltpu.get_barrier_semaphore()
    plane = [(mx, my) for my in (2, 3, 1, 0) for mx in (2, 1, 3, 0) if (mx, my) != (0, 0)]
    for mx, my in plane:
        pl.semaphore_signal(
            barrier, inc=1, device_id=place(flip(x, mx, 2), flip(y, my, 2), w), device_id_type=MESH
        )
    for m in range(1, 16):
        pl.semaphore_signal(
            barrier, inc=1, device_id=place(x, y, flip(w, m, 4)), device_id_type=MESH
        )

    def lanes(index):
        return pl.ds(pl.multiple_of(index * LANES, LANES), LANES)

    loads = []
    for index, (src, dst) in enumerate((
        (k_hbm, k_ref),
        (v_hbm, v_ref),
        (k_hbm.at[:, lanes(x)], kvb.at[x, :, pl.ds(0, LANES)]),
        (v_hbm.at[:, lanes(x)], kvb.at[x, :, pl.ds(LANES, LANES)]),
        (q_hbm.at[:, lanes(x)], qb.at[x]),
        (g_hbm.at[:, lanes(x)], gb.at[x]),
    )):
        copy = pltpu.make_async_copy(src, dst, loc.at[index])
        copy.start()
        loads.append(copy)
    pl.semaphore_wait(barrier, 30)

    def token_copies(mask):
        px = flip(x, mask, 2)
        device = place(px, y, w)
        pairs = (
            (k_hbm, kvb.at[x, :, pl.ds(0, LANES)]),
            (v_hbm, kvb.at[x, :, pl.ds(LANES, LANES)]),
            (q_hbm, qb.at[x]),
            (g_hbm, gb.at[x]),
        )
        return [
            remote(
                ref.at[:, lanes(px)], dst, p_send.at[i, mask - 1], p_recv.at[i, mask - 1], device
            )
            for i, (ref, dst) in enumerate(pairs)
        ]

    moves = {mask: token_copies(mask) for mask in (1, 2, 3)}
    moves[1][0].start()
    moves[3][0].start()

    for part, ref in ((0, k_ref), (1, v_ref)):
        loads[part].wait()
        rows = coarsen(coarsen(coarsen(coarsen(ref[...]))))
        for j in range(4):
            l4[j, :, part * LANES : (part + 1) * LANES] = rows[:, j * LANES : (j + 1) * LANES]
    stage_a = []
    for index, (mx, my) in enumerate(plane):
        copy = remote(
            l4.at[flip(x, mx, 2)], r4.at[y, x], a_send.at[index], a_recv.at[index],
            place(flip(x, mx, 2), flip(y, my, 2), w),
        )
        copy.start()
        stage_a.append(copy)

    for mask, i in ((1, 1), (3, 1), (2, 0), (2, 1)):
        moves[mask][i].start()
    for i in (2, 3):
        for mask in (1, 3, 2):
            moves[mask][i].start()
    r4[y, x] = l4[x]

    def chunk_forward(slot):
        q, kv = qb[slot], kvb[slot]
        weights, peak, weighted, total = attend(q, kv)
        w0[slot] = weights
        w0p[slot], w0w[slot], w0t[slot] = peak, weighted, total
        qp[slot] = coarsen(q)

    for copy in loads[2:5]:
        copy.wait()
    chunk_forward(x)
    kvp[x] = coarsen(kvb[x])

    for copy in stage_a:
        copy.wait_recv()
    half = pool_matrix(LANES)
    rows5 = coarsen(r4[...].reshape(256, 256))
    rows6 = coarsen(rows5)
    rows7 = coarsen(rows6)
    rows8 = coarsen(rows7)
    own5[...] = rows5.reshape(8, 16, 256)
    own6[...] = rows6.reshape(4, 16, 256)
    own7[...] = rows7.reshape(2, 16, 256)
    own8[...] = rows8.reshape(1, 16, 256)

    stage_b = []
    owns = (own5, own6, own7, own8)
    for m in range(15, 0, -1):
        up = m.bit_length() - 1
        count = 8 >> up
        start = 8 * up + (w % 2**up) * count
        copy = remote(
            owns[up], rf.at[pl.ds(start, count)], b_send.at[m - 1], b_recv.at[m - 1],
            place(x, y, flip(w, m, 4)),
        )
        copy.start()
        stage_b.append(copy)

    def unit_forward(unit, other):
        weights, peak, weighted, total = attend(qp[unit], kvp[other])
        w1[unit] = weights
        w1p[unit], w1w[unit], w1t[unit] = peak, weighted, total

    for mask in (1, 3, 2):
        for copy in moves[mask][:2]:
            copy.wait_recv()
        kvp[flip(x, mask, 2)] = coarsen(kvb[flip(x, mask, 2)])
    kvp[4] = coarsen(kvp[0:2].reshape(256, 256))
    kvp[5] = coarsen(kvp[2:4].reshape(256, 256))
    own3[...] = coarsen(kvp[4:6].reshape(256, 256))
    level3 = remote(own3, kv3sib, c_send.at[0], c_recv.at[0], place(x, sib, w))
    level3.start()
    for mask in (1, 3, 2):
        moves[mask][2].wait_recv()
        chunk_forward(flip(x, mask, 2))
        if mask == 1:
            unit_forward(x, flip(x, 1, 2))
            unit_forward(flip(x, 1, 2), x)
    qp[4] = coarsen(qp[0:2].reshape(256, LANES))
    qp[5] = coarsen(qp[2:4].reshape(256, LANES))
    qp[6] = coarsen(qp[4:6].reshape(256, LANES))
    unit_forward(flip(x, 3, 2), flip(x, 2, 2))
    unit_forward(flip(x, 2, 2), flip(x, 3, 2))
    unit_forward(4, 5)
    unit_forward(5, 4)
    level3.wait_recv()
    kvp[7] = kv3sib[...]
    unit_forward(6, 7)

    qs = mm(half, qp[6])
    qs = jnp.concatenate([qs, jnp.zeros((64, LANES), F32)], axis=0)
    shape = (LANES, LANES)
    row, col = iota(shape, 0), iota(shape, 1)
    down = jnp.where((row >= 64) & (shr(col, 1) == row - 64), 0.5, 0.0).astype(BF16)
    qs = qs.astype(BF16)
    upper_rows = iota((LANES, 1), 0) >= 64
    for _ in range(4):
        qs = jnp.where(upper_rows, mm(down, qs), qs.astype(F32)).astype(BF16)
    level = row_level(jnp.bitwise_and(iota((256, 1), 0), 127))

    for copy in stage_b:
        copy.wait_recv()
    far4 = r4[pl.ds(2 * (1 - y_pair), 2)].reshape(LANES, 256)
    far = jnp.concatenate([far4, rf[...].reshape(512, 256)], axis=0)
    far_vals = with_ones(far[:, LANES:])
    q_stack = stack_heads(qs)
    weights_s, peak_s = soft_weights(pick(mm_nt(q_stack, far[:, :LANES]), level))
    blocks_s = blocks_of(weights_s, level)
    both = mm(blocks_s, far_vals)
    weighted_s = fold(both[:, :LANES], LANES)
    total_s = fold(both[:, LANES:], LANES)
    peak_s = fold(jnp.broadcast_to(peak_s, (256, LANES)), LANES)

    spreads = level_spread()
    stats = jnp.concatenate(
        [peak_s.astype(BF16), *split2(weighted_s), *split2(total_s)], axis=1
    )
    taken = [mm(part.astype(BF16), stats) for part in spreads]
    m3 = w1p[6]
    for t in taken:
        m3 = jnp.maximum(m3, t[:, :LANES])
    a3 = jnp.exp(w1p[6] - m3)
    n3, d3 = a3 * w1w[6], a3 * w1t[6]
    shares_s = []
    for index, t in enumerate(taken):
        share = 2.0 ** (index + 1) * jnp.exp(t[:, :LANES] - m3)
        n3 = n3 + share * (t[:, 128:256] + t[:, 256:384])
        d3 = d3 + share * (t[:, 384:512] + t[:, 512:640])
        shares_s.append(share)

    used = [0]

    def fresh():
        used[0] += 1
        return sp.at[used[0] - 1]

    def doubled(values):
        count, ref = values.shape[0], fresh()
        ref[pl.ds(0, count, 2), :] = values
        ref[pl.ds(1, count, 2), :] = values
        return ref[0 : 2 * count, :]

    def paired(values):
        count, ref = values.shape[0], fresh()
        ref[0:count, :] = values
        return ref[pl.ds(0, count // 2, 2), :] + ref[pl.ds(1, count // 2, 2), :]

    def merge(peak, weighted, total, m, n, d):
        crest = jnp.maximum(peak, m)
        own = jnp.exp(peak - crest)
        rest = 2.0 * jnp.exp(m - crest)
        return crest, own * weighted + rest * n, own * total + rest * d, own, rest

    m2, n2, d2, own2, rest2 = merge(
        w1p[4:6].reshape(256, LANES), w1w[4:6].reshape(256, LANES), w1t[4:6].reshape(256, LANES),
        doubled(m3), doubled(n3), doubled(d3),
    )
    crest1, n1v, d1v, own1, rest1 = merge(
        w1p[0:4].reshape(512, LANES), w1w[0:4].reshape(512, LANES), w1t[0:4].reshape(512, LANES),
        doubled(m2), doubled(n2), doubled(d2),
    )
    m1[...] = crest1.reshape(4, LANES, LANES)
    n1[...] = n1v.reshape(4, LANES, LANES)
    d1[...] = d1v.reshape(4, LANES, LANES)

    same = jnp.where(shr(iota(shape, 0), 6) == shr(iota(shape, 1), 6), 1.0, 0.0).astype(BF16)
    head_sum = jnp.concatenate([same, same], axis=0)

    def output_copy(kind, mask):
        px = flip(x, mask, 2)
        if kind == 0:
            src, dst = ob.at[px], out_ref.at[:, lanes(x)]
        elif kind == 1:
            src, dst = oq.at[px], gq_ref.at[:, lanes(x)]
        else:
            src, dst = bk.at[px], bkr.at[x]
        return remote(
            src, dst, o_send.at[kind, mask - 1], o_recv.at[kind, mask - 1], place(px, y, w)
        )

    for mask in (1, 3, 2, 0):
        px = flip(x, mask, 2)
        crest, numer, denom, own, rest = merge(
            w0p[px], w0w[px], w0t[px], doubled(m1[px]), doubled(n1[px]), doubled(d1[px])
        )
        inverse = 1.0 / denom
        ratio = numer * inverse
        ob[px] = ratio.astype(BF16)
        ratios[mask], inverses[mask] = ratio, inverse
        w0p[px], w0t[px] = own, rest
    outs = {(kind, mask): output_copy(kind, mask) for kind in range(3) for mask in (1, 3, 2)}
    locals_ = [
        pltpu.make_async_copy(ob.at[x], out_ref.at[:, lanes(x)], loc.at[0]),
        pltpu.make_async_copy(oq.at[x], gq_ref.at[:, lanes(x)], loc.at[1]),
        pltpu.make_async_copy(bk.at[x], bkr.at[x], loc.at[2]),
        pltpu.make_async_copy(cs.at[x], cb.at[x], loc.at[3]),
    ]
    for mask in (1, 3, 2):
        outs[0, mask].start()
    locals_[0].start()

    for mask in (1, 3, 2):
        moves[mask][3].wait_recv()
    loads[5].wait()
    for mask in (1, 3, 2, 0):
        px = flip(x, mask, 2)
        up = gb[px].astype(F32)
        inverse = inverses[mask]
        high, low = split2(up * ratios[mask])
        drift = -mm(jnp.concatenate([high, low], axis=1), head_sum) * inverse
        scaled = up * inverse
        own, rest = w0p[px], w0t[px]
        gw0[px] = (own * scaled).astype(BF16)
        gt0[px] = own * drift
        g1s[px] = paired(rest * scaled)
        d1s[px] = paired(rest * drift)

    g1, dd1 = g1s[...].reshape(512, LANES), d1s[...].reshape(512, LANES)
    gw1[0:4] = (own1 * g1).astype(BF16).reshape(4, LANES, LANES)
    gt1[0:4] = (own1 * dd1).reshape(4, LANES, LANES)
    g2 = paired(rest1 * g1)
    dd2 = paired(rest1 * dd1)
    gw1[4:6] = (own2 * g2).astype(BF16).reshape(2, LANES, LANES)
    gt1[4:6] = (own2 * dd2).reshape(2, LANES, LANES)
    g3 = paired(rest2 * g2)
    dd3 = paired(rest2 * dd2)
    gw1[6] = (a3 * g3).astype(BF16)
    gt1[6] = a3 * dd3
    pieces = []
    for share in shares_s:
        pieces.append(
            jnp.concatenate([(share * g3).astype(BF16), *split2(share * dd3)], axis=1)
        )
    pooled = mm(level_pool(), jnp.concatenate(pieces, axis=0))
    gw_s = pooled[:, :LANES].astype(BF16)
    gt_s = pooled[:, 128:256] + pooled[:, 256:384]

    grads_s = stack_grads(gw_s, gt_s)
    lift = pick(mm_nt(grads_s, far_vals), level)
    gs = (weights_s.astype(F32) * lift).astype(BF16)
    gs_blocks = blocks_of(gs, level)
    gk_far = mm_tn(gs_blocks, q_stack)
    gv_far = mm_tn(blocks_s, grads_s[:, :LANES])
    far_grads = jnp.concatenate([gk_far, gv_far], axis=1)
    s4[...] = far_grads[:LANES].astype(BF16).reshape(2, 64, 256)
    sb[...] = far_grads[LANES:].astype(BF16).reshape(32, 16, 256)

    back_b = []
    for m in range(15, 0, -1):
        up = m.bit_length() - 1
        count = 8 >> up
        pw = flip(w, m, 4)
        theirs = 8 * up + (pw % 2**up) * count
        ours = 8 * up + (w % 2**up) * count
        copy = remote(
            sb.at[pl.ds(theirs, count)], rb.at[pl.ds(ours, count)],
            bb_send.at[m - 1], bb_recv.at[m - 1], place(x, y, pw),
        )
        copy.start()
        back_b.append(copy)

    gq_s = fold(mm(gs_blocks, far[:, :LANES]), LANES) * 0.125
    high, low = split2(gq_s)
    weighted_spread = spreads[0] * 0.5
    for index in range(1, 5):
        weighted_spread = weighted_spread + spreads[index] * 0.5 ** (index + 1)
    weighted_spread = weighted_spread.astype(BF16)
    run_q3 = mm(weighted_spread, high) + mm(weighted_spread, low)

    for unit in range(6, -1, -1):
        gq1[unit], gkv1[unit ^ 1] = attend_back(
            qp[unit], kvp[unit ^ 1], w1[unit], gw1[unit], gt1[unit]
        )

    s3[...] = gkv1[7].astype(BF16)
    back_y = [remote(s3, e3, ey_send.at[0], ey_recv.at[0], place(x, sib, w))]
    for m in (2, 3):
        py = flip(y, m, 2)
        back_y.append(
            remote(
                s4.at[py % 2], e4.at[y_bit], ey_send.at[m - 1], ey_recv.at[m - 1], place(x, py, w)
            )
        )
    for copy in back_y:
        copy.start()

    run_q2 = gq1[4:6].reshape(256, LANES) + 0.5 * doubled(gq1[6] + run_q3)
    run_q1 = gq1[0:4].reshape(512, LANES) + 0.5 * doubled(run_q2)
    run_k2 = gkv1[4:6, :, :LANES].reshape(256, LANES)
    run_v2 = gkv1[4:6, :, LANES:].reshape(256, LANES)
    run_k1 = gkv1[0:4, :, :LANES].reshape(512, LANES) + 0.5 * doubled(run_k2)
    run_v1 = gkv1[0:4, :, LANES:].reshape(512, LANES) + 0.5 * doubled(run_v2)
    m1[...] = run_q1.reshape(4, LANES, LANES)
    n1[...] = run_k1.reshape(4, LANES, LANES)
    d1[...] = run_v1.reshape(4, LANES, LANES)

    for mask in (1, 3, 2, 0):
        px = flip(x, mask, 2)
        gq, gkv = attend_back(qb[px], kvb[px], w0[px], gw0[px], gt0[px])
        gq = (gq + 0.5 * doubled(m1[px])).astype(BF16)
        gk = (gkv[:, :LANES] + 0.5 * doubled(n1[px])).astype(BF16)
        gv = (gkv[:, LANES:] + 0.5 * doubled(d1[px])).astype(BF16)
        oq[px] = gq
        bk[px, :, :LANES] = gk
        bk[px, :, LANES:] = gv
        if mask:
            outs[1, mask].start()
            outs[2, mask].start()
    locals_[1].start()
    locals_[2].start()

    for copy in back_b:
        copy.wait_recv()
    shape = (LANES, LANES)
    row, col = iota(shape, 0), iota(shape, 1)
    gather = []
    for up in range(4):
        inside = jnp.bitwise_and(col, (LANES >> up) - 1)
        gather.append(jnp.where(shr(row, up) == inside, 0.5**up, 0.0))
    gather = jnp.concatenate(gather, axis=1).astype(BF16)
    s5[...] = mm(gather, rb[...].reshape(512, 256)).astype(BF16).reshape(4, 2, 16, 256)
    for m in (1, 2, 3):
        py = flip(y, m, 2)
        copy = remote(s5.at[py], e5.at[y], e5_send.at[m - 1], e5_recv.at[m - 1], place(x, py, w))
        copy.start()
        back_y.append(copy)
    e5[y] = s5[y]
    fill = [jnp.where(row == col, 1.0, 0.0)]
    inside = jnp.bitwise_and(col, 63)
    fill.append(jnp.where(shr(row, 1) == inside, 0.5, 0.0))
    inside = jnp.bitwise_and(col, 31)
    fill.append(jnp.where(shr(row, 2) == inside, 0.25, 0.0))
    fill = jnp.concatenate(fill, axis=1).astype(BF16)
    for copy in back_y:
        copy.wait_recv()
    rows = jnp.concatenate([e3[...], e4[...].reshape(LANES, 256), e5[...].reshape(LANES, 256)], axis=0)
    cs[...] = mm(fill, rows).astype(BF16).reshape(4, 2, 16, 256)
    back_x = []
    for m in (1, 3, 2):
        px = flip(x, m, 2)
        copy = remote(cs.at[px], cb.at[x], cx_send.at[m - 1], cx_recv.at[m - 1], place(px, y, w))
        copy.start()
        back_x.append(copy)
    locals_[3].start()

    for copy in back_x:
        copy.wait_recv()
    for copy in outs.values():
        copy.wait_recv()
    for copy in locals_:
        copy.wait()
    for copies in (
        stage_a, [level3], stage_b, back_b, back_y, back_x, outs.values(),
        *moves.values(),
    ):
        for copy in copies:
            copy.wait_send()


def finish(
    out_h, gq_h, cb_h, bkr_h, out_ref, gq_ref, gk_ref, gv_ref,
    out_v, gq_v, cb, bkr, gk_v, gv_v, sems, out_sems,
):
    moves = [
        pltpu.make_async_copy(src, dst, sems.at[i])
        for i, (src, dst) in enumerate(
            ((cb_h, cb), (bkr_h, bkr), (out_h, out_v), (gq_h, gq_v))
        )
    ]
    for copy in moves:
        copy.start()
    shape = (256, 32)
    last = jnp.where(shr(iota(shape, 0), 3) == iota(shape, 1), 0.125, 0.0).astype(BF16)
    moves[2].wait()
    moves[3].wait()
    writes = [
        pltpu.make_async_copy(out_v, out_ref, out_sems.at[0]),
        pltpu.make_async_copy(gq_v, gq_ref, out_sems.at[1]),
    ]
    for copy in writes:
        copy.start()
    moves[0].wait()
    moves[1].wait()
    for j in range(4):
        total = mm(last, cb[j].reshape(32, 256)) + bkr[j].astype(F32)
        gk_v[:, j * LANES : (j + 1) * LANES] = total[:, :LANES].astype(BF16)
        gv_v[:, j * LANES : (j + 1) * LANES] = total[:, LANES:].astype(BF16)
    for i, (src, dst) in enumerate(((gk_v, gk_ref), (gv_v, gv_ref))):
        copy = pltpu.make_async_copy(src, dst, out_sems.at[2 + i])
        copy.start()
        writes.append(copy)
    for copy in writes:
        copy.wait()


def shards(query, key_in, value_in, grad_out):
    rows, width = query.shape
    whole = jax.ShapeDtypeStruct((rows, width), BF16)

    def f32(*shape):
        return pltpu.VMEM(shape, F32)

    def b16(*shape):
        return pltpu.VMEM(shape, BF16)

    dma = pltpu.SemaphoreType.DMA
    scratch = [
        b16(256, 512), b16(256, 512),
        b16(4, 256, 128), b16(4, 256, 256), b16(4, 256, 128),
        b16(4, 16, 256), b16(128, 256), b16(128, 256), b16(4, 4, 16, 256),
        b16(8, 16, 256), b16(4, 16, 256), b16(2, 16, 256), b16(1, 16, 256),
        b16(32, 16, 256),
        b16(7, 128, 128), b16(8, 128, 256),
        b16(4, 512, 256), b16(7, 256, 128),
        f32(4, 256, 128), f32(4, 256, 128), f32(4, 256, 128),
        f32(7, 128, 128), f32(7, 128, 128), f32(7, 128, 128),
        f32(4, 128, 128), f32(4, 128, 128), f32(4, 128, 128),
        b16(4, 256, 128), f32(4, 256, 128), b16(7, 128, 128), f32(7, 128, 128),
        f32(48, 512, 128), f32(4, 128, 128), f32(4, 128, 128),
        b16(4, 256, 128), b16(4, 256, 128), b16(4, 256, 256),
        f32(7, 128, 128), f32(8, 128, 256),
        b16(32, 16, 256), b16(32, 16, 256),
        b16(128, 256), b16(2, 64, 256), b16(4, 2, 16, 256),
        b16(128, 256), b16(2, 64, 256), b16(4, 2, 16, 256),
        b16(4, 2, 16, 256), f32(4, 256, 128), f32(4, 256, 128),
        dma((4, 3)), dma((4, 3)), dma((15,)), dma((15,)),
        dma((1,)), dma((1,)), dma((15,)), dma((15,)), dma((15,)), dma((15,)),
        dma((3,)), dma((3,)), dma((3,)), dma((3,)), dma((3,)), dma((3,)),
        dma((3, 3)), dma((3, 3)), dma((6,)),
    ]
    hbm = pl.BlockSpec(memory_space=pltpu.HBM)
    parts = pl.pallas_call(
        kernel,
        out_shape=(
            whole, whole,
            jax.ShapeDtypeStruct((4, 2, 16, 256), BF16), jax.ShapeDtypeStruct((4, 256, 256), BF16),
        ),
        in_specs=[hbm] * 4,
        out_specs=(hbm,) * 4,
        scratch_shapes=scratch,
        compiler_params=pltpu.CompilerParams(
            collective_id=0, has_side_effects=True, vmem_limit_bytes=56 * 2**20
        ),
    )(query, key_in, value_in, grad_out)
    return pl.pallas_call(
        finish,
        out_shape=(whole,) * 4,
        in_specs=[hbm] * 4,
        out_specs=(hbm,) * 4,
        scratch_shapes=[
            b16(256, 512), b16(256, 512), b16(4, 2, 16, 256), b16(4, 256, 256),
            b16(256, 512), b16(256, 512), dma((4,)), dma((4,)),
        ],
        compiler_params=pltpu.CompilerParams(vmem_limit_bytes=56 * 2**20),
    )(*parts)


def solution(mesh):
    spec = P(("grp", "seq"), None)
    return jax.shard_map(
        shards, mesh=mesh, in_specs=(spec,) * 4, out_specs=(spec,) * 4, check_vma=False
    )
```

```python
import functools

import jax
import jax.numpy as jnp
from jax import lax
from jax.experimental import pallas as pl
from jax.experimental.pallas import tpu as pltpu
from jax.sharding import PartitionSpec as P

MESH = pl.DeviceIdType.MESH
F32 = jnp.float32
BF16 = jnp.bfloat16
LANES = 128
NT = (((1,), (1,)), ((), ()))
TN = (((0,), (0,)), ((), ()))


def flip(value, mask, bits):
    out = 0
    for bit in range(bits):
        own = (value // 2**bit) % 2
        if isinstance(mask, int):
            out = out + 2**bit * (1 - own if (mask >> bit) & 1 else own)
        else:
            out = out + 2**bit * ((own + (mask // 2**bit) % 2) % 2)
    return out


def iota(shape, dim):
    return lax.broadcasted_iota(jnp.int32, shape, dim)


def shr(value, amount):
    return jnp.right_shift(value, amount)


def mm(a, b):
    return jnp.dot(a, b, preferred_element_type=F32)


def mm_nt(a, b):
    return lax.dot_general(a, b, NT, preferred_element_type=F32)


def mm_tn(a, b):
    return lax.dot_general(a, b, TN, preferred_element_type=F32)


def pool_matrix(rows, weight=0.5):
    shape = (rows // 2, rows)
    return jnp.where(shr(iota(shape, 1), 1) == iota(shape, 0), weight, 0.0).astype(BF16)


def spread_matrix(rows, weight):
    shape = (2 * rows, rows)
    return jnp.where(shr(iota(shape, 0), 1) == iota(shape, 1), weight, 0.0).astype(BF16)


def coarsen(values):
    return mm(pool_matrix(values.shape[0]), values).astype(BF16)


def lane_low():
    return iota((1, LANES), 1) < 64


def head_masks(weight):
    low = lane_low()
    return (
        jnp.where(low, weight, 0.0).astype(BF16),
        jnp.where(low, 0.0, weight).astype(BF16),
    )


def with_ones(vals):
    return jnp.concatenate([vals, jnp.ones_like(vals)], axis=1)


def fold(stacked, rows):
    return jnp.where(lane_low(), stacked[:rows], stacked[rows:])


def split2(values):
    high = values.astype(BF16)
    return high, (values - high.astype(F32)).astype(BF16)


def stack_heads(q):
    low, high = head_masks(0.125)
    return jnp.concatenate([q * low, q * high], axis=0)


def soft_weights(scores):
    peak = jnp.max(scores, axis=1, keepdims=True).astype(BF16).astype(F32)
    return jnp.exp(scores - peak).astype(BF16), peak


def attend(q, kv):
    rows = q.shape[0]
    scores = mm_nt(stack_heads(q), kv[:, :LANES])
    weights, peak = soft_weights(scores)
    both = mm(weights, with_ones(kv[:, LANES:]))
    weighted = fold(both[:, :LANES], rows)
    total = fold(both[:, LANES:], rows)
    wide = jnp.broadcast_to(peak, (2 * rows, LANES))
    return weights, fold(wide, rows), weighted, total


def stack_grads(gw, gt):
    low, high = head_masks(1.0)
    lane = iota((1, LANES), 1)
    first = jnp.where((lane == 0) | (lane == 64), 1.0, 0.0).astype(BF16)
    second = jnp.where((lane == 1) | (lane == 65), 1.0, 0.0).astype(BF16)
    gt_high, gt_low = split2(gt)
    extra = gt_high * first + gt_low * second
    return jnp.concatenate(
        [
            jnp.concatenate([gw * low, extra * low], axis=1),
            jnp.concatenate([gw * high, extra * high], axis=1),
        ],
        axis=0,
    )


def attend_back(q, kv, weights, gw, gt):
    rows = q.shape[0]
    stacked = stack_grads(gw, gt)
    lift = mm_nt(stacked, with_ones(kv[:, LANES:]))
    gs = (weights.astype(F32) * lift).astype(BF16)
    gv = mm_tn(weights, stacked[:, :LANES])
    gk = mm_tn(gs, stack_heads(q))
    gq = fold(mm(gs, kv[:, :LANES]), rows) * 0.125
    return gq, jnp.concatenate([gk, gv], axis=1)


OFFS = (0, 64, 96, 112, 120)


def row_level(row):
    level = jnp.zeros_like(row)
    for edge in OFFS[1:]:
        level = level + jnp.where(row >= edge, 1, 0)
    return level


def pick(full, level, width=LANES):
    out = jnp.where(level == 0, full[:, :width], 0.0)
    for index in range(1, 5):
        out = jnp.where(level == index, full[:, index * width : (index + 1) * width], out)
    return out


def blocks_of(values, level):
    zero = jnp.zeros_like(values)
    return jnp.concatenate([jnp.where(level == i, values, zero) for i in range(5)], axis=1)


def level_spread():
    parts = []
    shape = (LANES, LANES)
    row, col = iota(shape, 0), iota(shape, 1)
    for index, start in enumerate(OFFS):
        parts.append(jnp.where(col == start + shr(row, index + 1), 1.0, 0.0))
    return parts


def level_pool():
    parts = []
    shape = (LANES, LANES)
    row, col = iota(shape, 0), iota(shape, 1)
    for index, start in enumerate(OFFS):
        parts.append(jnp.where(row == start + shr(col, index + 1), 1.0, 0.0))
    return jnp.concatenate(parts, axis=1).astype(BF16)


def kernel(
    q_hbm, k_hbm, v_hbm, g_hbm, out_ref, gq_ref, cb, bkr, bvr,
    k_ref, v_ref, qb, kvb, gb, l4, own3, kv3sib, r4, own5, own6, own7, own8, rf,
    qp, kvp, w0, w1, w0w, w0p, w0t, w1w, w1p, w1t,
    m1, n1, d1, gw0, gt0, gw1, gt1, sp, g1s, d1s,
    ob, oq, bk, bv, gq1, gkv1, sb, rb, s3, s4, s5, e3, e4, e5, cs, ratios, inverses,
    p_send, p_recv, a_send, a_recv, c_send, c_recv, b_send, b_recv, bb_send, bb_recv,
    ey_send, ey_recv, e5_send, e5_recv, cx_send, cx_recv, o_send, o_recv, loc,
):
    grp, seq = lax.axis_index("grp"), lax.axis_index("seq")
    x, y = seq % 4, (seq // 4) % 4
    w = grp * 2 + seq // 16
    y_pair, y_bit = y // 2, y % 2
    sib = flip(y, 1, 2)

    def place(px, py, pw):
        return (pw // 2, (pw % 2) * 16 + py * 4 + px)

    def remote(src, dst, send, recv, device):
        return pltpu.make_async_remote_copy(
            src_ref=src, dst_ref=dst, send_sem=send, recv_sem=recv,
            device_id=device, device_id_type=MESH,
        )

    barrier = pltpu.get_barrier_semaphore()
    plane = [(mx, my) for my in (2, 3, 1, 0) for mx in (2, 1, 3, 0) if (mx, my) != (0, 0)]
    for mx, my in plane:
        pl.semaphore_signal(
            barrier, inc=1, device_id=place(flip(x, mx, 2), flip(y, my, 2), w), device_id_type=MESH
        )
    for m in range(1, 16):
        pl.semaphore_signal(
            barrier, inc=1, device_id=place(x, y, flip(w, m, 4)), device_id_type=MESH
        )

    def lanes(index):
        return pl.ds(pl.multiple_of(index * LANES, LANES), LANES)

    loads = []
    for index, (src, dst) in enumerate((
        (k_hbm, k_ref),
        (v_hbm, v_ref),
        (k_hbm.at[:, lanes(x)], kvb.at[x, :, pl.ds(0, LANES)]),
        (v_hbm.at[:, lanes(x)], kvb.at[x, :, pl.ds(LANES, LANES)]),
        (q_hbm.at[:, lanes(x)], qb.at[x]),
        (g_hbm.at[:, lanes(x)], gb.at[x]),
    )):
        copy = pltpu.make_async_copy(src, dst, loc.at[index])
        copy.start()
        loads.append(copy)
    pl.semaphore_wait(barrier, 30)

    def token_copies(mask):
        px = flip(x, mask, 2)
        device = place(px, y, w)
        pairs = (
            (k_hbm, kvb.at[x, :, pl.ds(0, LANES)]),
            (v_hbm, kvb.at[x, :, pl.ds(LANES, LANES)]),
            (q_hbm, qb.at[x]),
            (g_hbm, gb.at[x]),
        )
        return [
            remote(
                ref.at[:, lanes(px)], dst, p_send.at[i, mask - 1], p_recv.at[i, mask - 1], device
            )
            for i, (ref, dst) in enumerate(pairs)
        ]

    moves = {mask: token_copies(mask) for mask in (1, 2, 3)}
    moves[1][0].start()
    moves[3][0].start()

    for part, ref in ((0, k_ref), (1, v_ref)):
        loads[part].wait()
        rows = coarsen(coarsen(coarsen(coarsen(ref[...]))))
        for j in range(4):
            l4[j, :, part * LANES : (part + 1) * LANES] = rows[:, j * LANES : (j + 1) * LANES]
    stage_a = []
    for index, (mx, my) in enumerate(plane):
        copy = remote(
            l4.at[flip(x, mx, 2)], r4.at[y, x], a_send.at[index], a_recv.at[index],
            place(flip(x, mx, 2), flip(y, my, 2), w),
        )
        copy.start()
        stage_a.append(copy)

    for mask, i in ((1, 1), (3, 1), (2, 0), (2, 1)):
        moves[mask][i].start()
    for i in (2, 3):
        for mask in (1, 3, 2):
            moves[mask][i].start()
    r4[y, x] = l4[x]

    def chunk_forward(slot):
        q, kv = qb[slot], kvb[slot]
        weights, peak, weighted, total = attend(q, kv)
        w0[slot] = weights
        w0p[slot], w0w[slot], w0t[slot] = peak, weighted, total
        qp[slot] = coarsen(q)

    for copy in loads[2:5]:
        copy.wait()
    chunk_forward(x)
    kvp[x] = coarsen(kvb[x])

    for copy in stage_a:
        copy.wait_recv()
    half = pool_matrix(LANES)
    rows5 = coarsen(r4[...].reshape(256, 256))
    rows6 = coarsen(rows5)
    rows7 = coarsen(rows6)
    rows8 = coarsen(rows7)
    own5[...] = rows5.reshape(8, 16, 256)
    own6[...] = rows6.reshape(4, 16, 256)
    own7[...] = rows7.reshape(2, 16, 256)
    own8[...] = rows8.reshape(1, 16, 256)

    stage_b = []
    owns = (own5, own6, own7, own8)
    for m in range(15, 0, -1):
        up = m.bit_length() - 1
        count = 8 >> up
        start = 8 * up + (w % 2**up) * count
        copy = remote(
            owns[up], rf.at[pl.ds(start, count)], b_send.at[m - 1], b_recv.at[m - 1],
            place(x, y, flip(w, m, 4)),
        )
        copy.start()
        stage_b.append(copy)

    def unit_forward(unit, other):
        weights, peak, weighted, total = attend(qp[unit], kvp[other])
        w1[unit] = weights
        w1p[unit], w1w[unit], w1t[unit] = peak, weighted, total

    for mask in (1, 3, 2):
        for copy in moves[mask][:2]:
            copy.wait_recv()
        kvp[flip(x, mask, 2)] = coarsen(kvb[flip(x, mask, 2)])
    kvp[4] = coarsen(kvp[0:2].reshape(256, 256))
    kvp[5] = coarsen(kvp[2:4].reshape(256, 256))
    own3[...] = coarsen(kvp[4:6].reshape(256, 256))
    level3 = remote(own3, kv3sib, c_send.at[0], c_recv.at[0], place(x, sib, w))
    level3.start()
    for mask in (1, 3, 2):
        moves[mask][2].wait_recv()
        chunk_forward(flip(x, mask, 2))
        if mask == 1:
            unit_forward(x, flip(x, 1, 2))
            unit_forward(flip(x, 1, 2), x)
    qp[4] = coarsen(qp[0:2].reshape(256, LANES))
    qp[5] = coarsen(qp[2:4].reshape(256, LANES))
    qp[6] = coarsen(qp[4:6].reshape(256, LANES))
    unit_forward(flip(x, 3, 2), flip(x, 2, 2))
    unit_forward(flip(x, 2, 2), flip(x, 3, 2))
    unit_forward(4, 5)
    unit_forward(5, 4)
    level3.wait_recv()
    kvp[7] = kv3sib[...]
    unit_forward(6, 7)

    qs = mm(half, qp[6])
    qs = jnp.concatenate([qs, jnp.zeros((64, LANES), F32)], axis=0)
    shape = (LANES, LANES)
    row, col = iota(shape, 0), iota(shape, 1)
    down = jnp.where((row >= 64) & (shr(col, 1) == row - 64), 0.5, 0.0).astype(BF16)
    qs = qs.astype(BF16)
    upper_rows = iota((LANES, 1), 0) >= 64
    for _ in range(4):
        qs = jnp.where(upper_rows, mm(down, qs), qs.astype(F32)).astype(BF16)
    level = row_level(jnp.bitwise_and(iota((256, 1), 0), 127))

    for copy in stage_b:
        copy.wait_recv()
    far4 = r4[pl.ds(2 * (1 - y_pair), 2)].reshape(LANES, 256)
    far = jnp.concatenate([far4, rf[...].reshape(512, 256)], axis=0)
    far_vals = with_ones(far[:, LANES:])
    q_stack = stack_heads(qs)
    weights_s, peak_s = soft_weights(pick(mm_nt(q_stack, far[:, :LANES]), level))
    blocks_s = blocks_of(weights_s, level)
    both = mm(blocks_s, far_vals)
    weighted_s = fold(both[:, :LANES], LANES)
    total_s = fold(both[:, LANES:], LANES)
    peak_s = fold(jnp.broadcast_to(peak_s, (256, LANES)), LANES)

    spreads = level_spread()
    stats = jnp.concatenate(
        [peak_s.astype(BF16), *split2(weighted_s), *split2(total_s)], axis=1
    )
    taken = [mm(part.astype(BF16), stats) for part in spreads]
    m3 = w1p[6]
    for t in taken:
        m3 = jnp.maximum(m3, t[:, :LANES])
    a3 = jnp.exp(w1p[6] - m3)
    n3, d3 = a3 * w1w[6], a3 * w1t[6]
    shares_s = []
    for index, t in enumerate(taken):
        share = 2.0 ** (index + 1) * jnp.exp(t[:, :LANES] - m3)
        n3 = n3 + share * (t[:, 128:256] + t[:, 256:384])
        d3 = d3 + share * (t[:, 384:512] + t[:, 512:640])
        shares_s.append(share)

    used = [0]

    def fresh():
        used[0] += 1
        return sp.at[used[0] - 1]

    def doubled(values):
        count, ref = values.shape[0], fresh()
        ref[pl.ds(0, count, 2), :] = values
        ref[pl.ds(1, count, 2), :] = values
        return ref[0 : 2 * count, :]

    def paired(values):
        count, ref = values.shape[0], fresh()
        ref[0:count, :] = values
        return ref[pl.ds(0, count // 2, 2), :] + ref[pl.ds(1, count // 2, 2), :]

    def merge(peak, weighted, total, m, n, d):
        crest = jnp.maximum(peak, m)
        own = jnp.exp(peak - crest)
        rest = 2.0 * jnp.exp(m - crest)
        return crest, own * weighted + rest * n, own * total + rest * d, own, rest

    m2, n2, d2, own2, rest2 = merge(
        w1p[4:6].reshape(256, LANES), w1w[4:6].reshape(256, LANES), w1t[4:6].reshape(256, LANES),
        doubled(m3), doubled(n3), doubled(d3),
    )
    crest1, n1v, d1v, own1, rest1 = merge(
        w1p[0:4].reshape(512, LANES), w1w[0:4].reshape(512, LANES), w1t[0:4].reshape(512, LANES),
        doubled(m2), doubled(n2), doubled(d2),
    )
    m1[...] = crest1.reshape(4, LANES, LANES)
    n1[...] = n1v.reshape(4, LANES, LANES)
    d1[...] = d1v.reshape(4, LANES, LANES)

    same = jnp.where(shr(iota(shape, 0), 6) == shr(iota(shape, 1), 6), 1.0, 0.0).astype(BF16)
    head_sum = jnp.concatenate([same, same], axis=0)

    def output_copy(kind, mask):
        px = flip(x, mask, 2)
        if kind == 0:
            src, dst = ob.at[px], out_ref.at[:, lanes(x)]
        elif kind == 1:
            src, dst = oq.at[px], gq_ref.at[:, lanes(x)]
        elif kind == 2:
            src, dst = bk.at[px], bkr.at[x]
        else:
            src, dst = bv.at[px], bvr.at[x]
        return remote(
            src, dst, o_send.at[kind, mask - 1], o_recv.at[kind, mask - 1], place(px, y, w)
        )

    for mask in (1, 3, 2, 0):
        px = flip(x, mask, 2)
        crest, numer, denom, own, rest = merge(
            w0p[px], w0w[px], w0t[px], doubled(m1[px]), doubled(n1[px]), doubled(d1[px])
        )
        inverse = 1.0 / denom
        ratio = numer * inverse
        ob[px] = ratio.astype(BF16)
        ratios[mask], inverses[mask] = ratio, inverse
        w0p[px], w0t[px] = own, rest
    outs = {(kind, mask): output_copy(kind, mask) for kind in range(4) for mask in (1, 3, 2)}
    locals_ = [
        pltpu.make_async_copy(ob.at[x], out_ref.at[:, lanes(x)], loc.at[0]),
        pltpu.make_async_copy(oq.at[x], gq_ref.at[:, lanes(x)], loc.at[1]),
        pltpu.make_async_copy(bk.at[x], bkr.at[x], loc.at[2]),
        pltpu.make_async_copy(cs.at[x], cb.at[x], loc.at[3]),
        pltpu.make_async_copy(bv.at[x], bvr.at[x], loc.at[4]),
    ]
    for mask in (1, 3, 2):
        outs[0, mask].start()
    locals_[0].start()

    for mask in (1, 3, 2):
        moves[mask][3].wait_recv()
    loads[5].wait()
    for mask in (1, 3, 2, 0):
        px = flip(x, mask, 2)
        up = gb[px].astype(F32)
        inverse = inverses[mask]
        high, low = split2(up * ratios[mask])
        drift = -mm(jnp.concatenate([high, low], axis=1), head_sum) * inverse
        scaled = up * inverse
        own, rest = w0p[px], w0t[px]
        gw0[px] = (own * scaled).astype(BF16)
        gt0[px] = own * drift
        g1s[px] = paired(rest * scaled)
        d1s[px] = paired(rest * drift)

    g1, dd1 = g1s[...].reshape(512, LANES), d1s[...].reshape(512, LANES)
    gw1[0:4] = (own1 * g1).astype(BF16).reshape(4, LANES, LANES)
    gt1[0:4] = (own1 * dd1).reshape(4, LANES, LANES)
    g2 = paired(rest1 * g1)
    dd2 = paired(rest1 * dd1)
    gw1[4:6] = (own2 * g2).astype(BF16).reshape(2, LANES, LANES)
    gt1[4:6] = (own2 * dd2).reshape(2, LANES, LANES)
    g3 = paired(rest2 * g2)
    dd3 = paired(rest2 * dd2)
    gw1[6] = (a3 * g3).astype(BF16)
    gt1[6] = a3 * dd3
    pieces = []
    for share in shares_s:
        pieces.append(
            jnp.concatenate([(share * g3).astype(BF16), *split2(share * dd3)], axis=1)
        )
    pooled = mm(level_pool(), jnp.concatenate(pieces, axis=0))
    gw_s = pooled[:, :LANES].astype(BF16)
    gt_s = pooled[:, 128:256] + pooled[:, 256:384]

    grads_s = stack_grads(gw_s, gt_s)
    lift = pick(mm_nt(grads_s, far_vals), level)
    gs = (weights_s.astype(F32) * lift).astype(BF16)
    gs_blocks = blocks_of(gs, level)
    gk_far = mm_tn(gs_blocks, q_stack)
    gv_far = mm_tn(blocks_s, grads_s[:, :LANES])
    far_grads = jnp.concatenate([gk_far, gv_far], axis=1)
    s4[...] = far_grads[:LANES].astype(BF16).reshape(2, 64, 256)
    sb[...] = far_grads[LANES:].astype(BF16).reshape(32, 16, 256)

    back_b = []
    for m in range(15, 0, -1):
        up = m.bit_length() - 1
        count = 8 >> up
        pw = flip(w, m, 4)
        theirs = 8 * up + (pw % 2**up) * count
        ours = 8 * up + (w % 2**up) * count
        copy = remote(
            sb.at[pl.ds(theirs, count)], rb.at[pl.ds(ours, count)],
            bb_send.at[m - 1], bb_recv.at[m - 1], place(x, y, pw),
        )
        copy.start()
        back_b.append(copy)

    gq_s = fold(mm(gs_blocks, far[:, :LANES]), LANES) * 0.125
    high, low = split2(gq_s)
    weighted_spread = spreads[0] * 0.5
    for index in range(1, 5):
        weighted_spread = weighted_spread + spreads[index] * 0.5 ** (index + 1)
    weighted_spread = weighted_spread.astype(BF16)
    run_q3 = mm(weighted_spread, high) + mm(weighted_spread, low)

    for unit in range(6, -1, -1):
        gq1[unit], gkv1[unit ^ 1] = attend_back(
            qp[unit], kvp[unit ^ 1], w1[unit], gw1[unit], gt1[unit]
        )

    s3[...] = gkv1[7].astype(BF16)
    back_y = [remote(s3, e3, ey_send.at[0], ey_recv.at[0], place(x, sib, w))]
    for m in (2, 3):
        py = flip(y, m, 2)
        back_y.append(
            remote(
                s4.at[py % 2], e4.at[y_bit], ey_send.at[m - 1], ey_recv.at[m - 1], place(x, py, w)
            )
        )
    for copy in back_y:
        copy.start()

    run_q2 = gq1[4:6].reshape(256, LANES) + 0.5 * doubled(gq1[6] + run_q3)
    run_q1 = gq1[0:4].reshape(512, LANES) + 0.5 * doubled(run_q2)
    run_k2 = gkv1[4:6, :, :LANES].reshape(256, LANES)
    run_v2 = gkv1[4:6, :, LANES:].reshape(256, LANES)
    run_k1 = gkv1[0:4, :, :LANES].reshape(512, LANES) + 0.5 * doubled(run_k2)
    run_v1 = gkv1[0:4, :, LANES:].reshape(512, LANES) + 0.5 * doubled(run_v2)
    m1[...] = run_q1.reshape(4, LANES, LANES)
    n1[...] = run_k1.reshape(4, LANES, LANES)
    d1[...] = run_v1.reshape(4, LANES, LANES)

    for mask in (1, 3, 2, 0):
        px = flip(x, mask, 2)
        gq, gkv = attend_back(qb[px], kvb[px], w0[px], gw0[px], gt0[px])
        gq = (gq + 0.5 * doubled(m1[px])).astype(BF16)
        gk = (gkv[:, :LANES] + 0.5 * doubled(n1[px])).astype(BF16)
        gv = (gkv[:, LANES:] + 0.5 * doubled(d1[px])).astype(BF16)
        oq[px] = gq
        bk[px] = gk
        bv[px] = gv
        if mask:
            outs[1, mask].start()
            outs[2, mask].start()
            outs[3, mask].start()
    locals_[1].start()
    locals_[2].start()
    locals_[4].start()

    for copy in back_b:
        copy.wait_recv()
    shape = (LANES, LANES)
    row, col = iota(shape, 0), iota(shape, 1)
    gather = []
    for up in range(4):
        inside = jnp.bitwise_and(col, (LANES >> up) - 1)
        gather.append(jnp.where(shr(row, up) == inside, 0.5**up, 0.0))
    gather = jnp.concatenate(gather, axis=1).astype(BF16)
    s5[...] = mm(gather, rb[...].reshape(512, 256)).astype(BF16).reshape(4, 2, 16, 256)
    for m in (1, 2, 3):
        py = flip(y, m, 2)
        copy = remote(s5.at[py], e5.at[y], e5_send.at[m - 1], e5_recv.at[m - 1], place(x, py, w))
        copy.start()
        back_y.append(copy)
    e5[y] = s5[y]
    fill = [jnp.where(row == col, 1.0, 0.0)]
    inside = jnp.bitwise_and(col, 63)
    fill.append(jnp.where(shr(row, 1) == inside, 0.5, 0.0))
    inside = jnp.bitwise_and(col, 31)
    fill.append(jnp.where(shr(row, 2) == inside, 0.25, 0.0))
    fill = jnp.concatenate(fill, axis=1).astype(BF16)
    for copy in back_y:
        copy.wait_recv()
    rows = jnp.concatenate([e3[...], e4[...].reshape(LANES, 256), e5[...].reshape(LANES, 256)], axis=0)
    cs[...] = mm(fill, rows).astype(BF16).reshape(4, 2, 16, 256)
    back_x = []
    for m in (1, 3, 2):
        px = flip(x, m, 2)
        copy = remote(cs.at[px], cb.at[x], cx_send.at[m - 1], cx_recv.at[m - 1], place(px, y, w))
        copy.start()
        back_x.append(copy)
    locals_[3].start()

    for copy in back_x:
        copy.wait_recv()
    for copy in outs.values():
        copy.wait_recv()
    for copy in locals_:
        copy.wait()
    for copies in (
        stage_a, [level3], stage_b, back_b, back_y, back_x, outs.values(),
        *moves.values(),
    ):
        for copy in copies:
            copy.wait_send()


def finish(out_v, gq_v, cb, bk, bv, out_ref, gq_ref, gk_ref, gv_ref, gk_v, gv_v, sems):
    writes = [
        pltpu.make_async_copy(out_v, out_ref, sems.at[0]),
        pltpu.make_async_copy(gq_v, gq_ref, sems.at[1]),
    ]
    for copy in writes:
        copy.start()
    shape = (256, 32)
    last = jnp.where(shr(iota(shape, 0), 3) == iota(shape, 1), 0.125, 0.0).astype(BF16)
    for j in range(4):
        total = mm(last, cb[j].reshape(32, 256))
        gk_v[:, j * LANES : (j + 1) * LANES] = (total[:, :LANES] + bk[j].astype(F32)).astype(BF16)
        gv_v[:, j * LANES : (j + 1) * LANES] = (total[:, LANES:] + bv[j].astype(F32)).astype(BF16)
    for i, (src, dst) in enumerate(((gk_v, gk_ref), (gv_v, gv_ref))):
        copy = pltpu.make_async_copy(src, dst, sems.at[2 + i])
        copy.start()
        writes.append(copy)
    for copy in writes:
        copy.wait()


def shards(query, key_in, value_in, grad_out):
    rows, width = query.shape
    whole = jax.ShapeDtypeStruct((rows, width), BF16)

    def f32(*shape):
        return pltpu.VMEM(shape, F32)

    def b16(*shape):
        return pltpu.VMEM(shape, BF16)

    dma = pltpu.SemaphoreType.DMA
    scratch = [
        b16(256, 512), b16(256, 512),
        b16(4, 256, 128), b16(4, 256, 256), b16(4, 256, 128),
        b16(4, 16, 256), b16(128, 256), b16(128, 256), b16(4, 4, 16, 256),
        b16(8, 16, 256), b16(4, 16, 256), b16(2, 16, 256), b16(1, 16, 256),
        b16(32, 16, 256),
        b16(7, 128, 128), b16(8, 128, 256),
        b16(4, 512, 256), b16(7, 256, 128),
        f32(4, 256, 128), f32(4, 256, 128), f32(4, 256, 128),
        f32(7, 128, 128), f32(7, 128, 128), f32(7, 128, 128),
        f32(4, 128, 128), f32(4, 128, 128), f32(4, 128, 128),
        b16(4, 256, 128), f32(4, 256, 128), b16(7, 128, 128), f32(7, 128, 128),
        f32(48, 512, 128), f32(4, 128, 128), f32(4, 128, 128),
        b16(4, 256, 128), b16(4, 256, 128), b16(4, 256, 128), b16(4, 256, 128),
        f32(7, 128, 128), f32(8, 128, 256),
        b16(32, 16, 256), b16(32, 16, 256),
        b16(128, 256), b16(2, 64, 256), b16(4, 2, 16, 256),
        b16(128, 256), b16(2, 64, 256), b16(4, 2, 16, 256),
        b16(4, 2, 16, 256), f32(4, 256, 128), f32(4, 256, 128),
        dma((4, 3)), dma((4, 3)), dma((15,)), dma((15,)),
        dma((1,)), dma((1,)), dma((15,)), dma((15,)), dma((15,)), dma((15,)),
        dma((3,)), dma((3,)), dma((3,)), dma((3,)), dma((3,)), dma((3,)),
        dma((4, 3)), dma((4, 3)), dma((6,)),
    ]
    hbm = pl.BlockSpec(memory_space=pltpu.HBM)
    vmem = pl.BlockSpec(memory_space=pltpu.VMEM)
    anywhere = pl.BlockSpec(memory_space=pl.ANY)
    parts = pl.pallas_call(
        kernel,
        out_shape=(
            whole, whole,
            jax.ShapeDtypeStruct((4, 2, 16, 256), BF16), *[jax.ShapeDtypeStruct((4, 256, 128), BF16)] * 2,
        ),
        in_specs=[hbm] * 4,
        out_specs=(anywhere,) * 5,
        scratch_shapes=scratch,
        compiler_params=pltpu.CompilerParams(
            collective_id=0, has_side_effects=True, vmem_limit_bytes=54036 * 2**10
        ),
    )(query, key_in, value_in, grad_out)
    return pl.pallas_call(
        finish,
        out_shape=(whole,) * 4,
        in_specs=[vmem] * 5,
        out_specs=(hbm,) * 4,
        scratch_shapes=[b16(256, 512), b16(256, 512), dma((4,))],
        compiler_params=pltpu.CompilerParams(vmem_limit_bytes=8 * 2**20),
    )(*parts)


def solution(mesh):
    spec = P(("grp", "seq"), None)
    return jax.shard_map(
        shards, mesh=mesh, in_specs=(spec,) * 4, out_specs=(spec,) * 4, check_vma=False
    )
```

```python
import functools

import jax
import jax.numpy as jnp
from jax import lax
from jax.experimental import pallas as pl
from jax.experimental.pallas import tpu as pltpu
from jax.sharding import PartitionSpec as P

MESH = pl.DeviceIdType.MESH
F32 = jnp.float32
BF16 = jnp.bfloat16
LANES = 128
NT = (((1,), (1,)), ((), ()))
TN = (((0,), (0,)), ((), ()))


def flip(value, mask, bits):
    out = 0
    for bit in range(bits):
        own = (value // 2**bit) % 2
        if isinstance(mask, int):
            out = out + 2**bit * (1 - own if (mask >> bit) & 1 else own)
        else:
            out = out + 2**bit * ((own + (mask // 2**bit) % 2) % 2)
    return out


def iota(shape, dim):
    return lax.broadcasted_iota(jnp.int32, shape, dim)


def shr(value, amount):
    return jnp.right_shift(value, amount)


def mm(a, b):
    return jnp.dot(a, b, preferred_element_type=F32)


def mm_nt(a, b):
    return lax.dot_general(a, b, NT, preferred_element_type=F32)


def mm_tn(a, b):
    return lax.dot_general(a, b, TN, preferred_element_type=F32)


def pool_matrix(rows, weight=0.5):
    shape = (rows // 2, rows)
    return jnp.where(shr(iota(shape, 1), 1) == iota(shape, 0), weight, 0.0).astype(BF16)


def spread_matrix(rows, weight):
    shape = (2 * rows, rows)
    return jnp.where(shr(iota(shape, 0), 1) == iota(shape, 1), weight, 0.0).astype(BF16)


def coarsen(values):
    return mm(pool_matrix(values.shape[0]), values).astype(BF16)


def lane_low():
    return iota((1, LANES), 1) < 64


def head_masks(weight):
    low = lane_low()
    return (
        jnp.where(low, weight, 0.0).astype(BF16),
        jnp.where(low, 0.0, weight).astype(BF16),
    )


def with_ones(vals):
    return jnp.concatenate([vals, jnp.ones_like(vals)], axis=1)


def fold(stacked, rows):
    return jnp.where(lane_low(), stacked[:rows], stacked[rows:])


def split2(values):
    high = values.astype(BF16)
    return high, (values - high.astype(F32)).astype(BF16)


def stack_heads(q):
    low, high = head_masks(0.125)
    return jnp.concatenate([q * low, q * high], axis=0)


def soft_weights(scores):
    peak = jnp.max(scores, axis=1, keepdims=True).astype(BF16).astype(F32)
    return jnp.exp(scores - peak).astype(BF16), peak


def attend(q, kv):
    rows = q.shape[0]
    scores = mm_nt(stack_heads(q), kv[:, :LANES])
    weights, peak = soft_weights(scores)
    both = mm(weights, with_ones(kv[:, LANES:]))
    weighted = fold(both[:, :LANES], rows)
    total = fold(both[:, LANES:], rows)
    wide = jnp.broadcast_to(peak, (2 * rows, LANES))
    return weights, fold(wide, rows), weighted, total


def stack_grads(gw, gt):
    low, high = head_masks(1.0)
    lane = iota((1, LANES), 1)
    first = jnp.where((lane == 0) | (lane == 64), 1.0, 0.0).astype(BF16)
    second = jnp.where((lane == 1) | (lane == 65), 1.0, 0.0).astype(BF16)
    gt_high, gt_low = split2(gt)
    extra = gt_high * first + gt_low * second
    return jnp.concatenate(
        [
            jnp.concatenate([gw * low, extra * low], axis=1),
            jnp.concatenate([gw * high, extra * high], axis=1),
        ],
        axis=0,
    )


def attend_back(q, kv, weights, gw, gt):
    rows = q.shape[0]
    stacked = stack_grads(gw, gt)
    lift = mm_nt(stacked, with_ones(kv[:, LANES:]))
    gs = (weights.astype(F32) * lift).astype(BF16)
    gv = mm_tn(weights, stacked[:, :LANES])
    gk = mm_tn(gs, stack_heads(q))
    gq = fold(mm(gs, kv[:, :LANES]), rows) * 0.125
    return gq, jnp.concatenate([gk, gv], axis=1)


OFFS = (0, 64, 96, 112, 120)


def row_level(row):
    level = jnp.zeros_like(row)
    for edge in OFFS[1:]:
        level = level + jnp.where(row >= edge, 1, 0)
    return level


def pick(full, level, width=LANES):
    out = jnp.where(level == 0, full[:, :width], 0.0)
    for index in range(1, 5):
        out = jnp.where(level == index, full[:, index * width : (index + 1) * width], out)
    return out


def blocks_of(values, level):
    zero = jnp.zeros_like(values)
    return jnp.concatenate([jnp.where(level == i, values, zero) for i in range(5)], axis=1)


def level_spread():
    parts = []
    shape = (LANES, LANES)
    row, col = iota(shape, 0), iota(shape, 1)
    for index, start in enumerate(OFFS):
        parts.append(jnp.where(col == start + shr(row, index + 1), 1.0, 0.0))
    return parts


def level_pool():
    parts = []
    shape = (LANES, LANES)
    row, col = iota(shape, 0), iota(shape, 1)
    for index, start in enumerate(OFFS):
        parts.append(jnp.where(row == start + shr(col, index + 1), 1.0, 0.0))
    return jnp.concatenate(parts, axis=1).astype(BF16)


def kernel(
    q_hbm, k_hbm, v_hbm, g_hbm, out_ref, gq_ref, cb, bkr, bvr,
    k_ref, v_ref, qb, kvb, gb, l4, own3, kv3sib, r4, own5, own6, own7, own8, rf,
    qp, kvp, w0, w1, w0w, w0p, w0t, w1w, w1p, w1t,
    m1, n1, d1, gw0, gt0, gw1, gt1, sp, g1s, d1s,
    ob, oq, bk, bv, gq1, gkv1, sb, rb, s3, s4, s5, e3, e4, e5, cs, ratios, inverses,
    p_send, p_recv, a_send, a_recv, c_send, c_recv, b_send, b_recv, bb_send, bb_recv,
    ey_send, ey_recv, e5_send, e5_recv, cx_send, cx_recv, o_send, o_recv, loc,
):
    grp, seq = lax.axis_index("grp"), lax.axis_index("seq")
    x, y = seq % 4, (seq // 4) % 4
    w = grp * 2 + seq // 16
    y_pair, y_bit = y // 2, y % 2
    sib = flip(y, 1, 2)

    def place(px, py, pw):
        return (pw // 2, (pw % 2) * 16 + py * 4 + px)

    def remote(src, dst, send, recv, device):
        return pltpu.make_async_remote_copy(
            src_ref=src, dst_ref=dst, send_sem=send, recv_sem=recv,
            device_id=device, device_id_type=MESH,
        )

    barrier = pltpu.get_barrier_semaphore()
    plane = [(mx, my) for my in (2, 3, 1, 0) for mx in (2, 1, 3, 0) if (mx, my) != (0, 0)]
    for mx, my in plane:
        pl.semaphore_signal(
            barrier, inc=1, device_id=place(flip(x, mx, 2), flip(y, my, 2), w), device_id_type=MESH
        )
    for m in range(1, 16):
        pl.semaphore_signal(
            barrier, inc=1, device_id=place(x, y, flip(w, m, 4)), device_id_type=MESH
        )

    def lanes(index):
        return pl.ds(pl.multiple_of(index * LANES, LANES), LANES)

    loads = []
    for index, (src, dst) in enumerate((
        (k_hbm, k_ref),
        (v_hbm, v_ref),
        (k_hbm.at[:, lanes(x)], kvb.at[x, :, pl.ds(0, LANES)]),
        (v_hbm.at[:, lanes(x)], kvb.at[x, :, pl.ds(LANES, LANES)]),
        (q_hbm.at[:, lanes(x)], qb.at[x]),
        (g_hbm.at[:, lanes(x)], gb.at[x]),
    )):
        copy = pltpu.make_async_copy(src, dst, loc.at[index])
        copy.start()
        loads.append(copy)
    pl.semaphore_wait(barrier, 30)

    def token_copies(mask):
        px = flip(x, mask, 2)
        device = place(px, y, w)
        pairs = (
            (k_hbm, kvb.at[x, :, pl.ds(0, LANES)]),
            (v_hbm, kvb.at[x, :, pl.ds(LANES, LANES)]),
            (q_hbm, qb.at[x]),
            (g_hbm, gb.at[x]),
        )
        return [
            remote(
                ref.at[:, lanes(px)], dst, p_send.at[i, mask - 1], p_recv.at[i, mask - 1], device
            )
            for i, (ref, dst) in enumerate(pairs)
        ]

    moves = {mask: token_copies(mask) for mask in (1, 2, 3)}
    moves[1][0].start()
    moves[3][0].start()

    for part, ref in ((0, k_ref), (1, v_ref)):
        loads[part].wait()
        rows = coarsen(coarsen(coarsen(coarsen(ref[...]))))
        for j in range(4):
            l4[j, :, part * LANES : (part + 1) * LANES] = rows[:, j * LANES : (j + 1) * LANES]
    stage_a = []
    for index, (mx, my) in enumerate(plane):
        copy = remote(
            l4.at[flip(x, mx, 2)], r4.at[y, x], a_send.at[index], a_recv.at[index],
            place(flip(x, mx, 2), flip(y, my, 2), w),
        )
        copy.start()
        stage_a.append(copy)

    for mask, i in ((1, 1), (3, 1), (2, 0), (2, 1)):
        moves[mask][i].start()
    for i in (2, 3):
        for mask in (1, 3, 2):
            moves[mask][i].start()
    r4[y, x] = l4[x]

    def chunk_forward(slot):
        q, kv = qb[slot], kvb[slot]
        weights, peak, weighted, total = attend(q, kv)
        w0[slot] = weights
        w0p[slot], w0w[slot], w0t[slot] = peak, weighted, total
        qp[slot] = coarsen(q)

    for copy in loads[2:5]:
        copy.wait()
    chunk_forward(x)
    kvp[x] = coarsen(kvb[x])

    for copy in stage_a:
        copy.wait_recv()
    half = pool_matrix(LANES)
    rows5 = coarsen(r4[...].reshape(256, 256))
    rows6 = coarsen(rows5)
    rows7 = coarsen(rows6)
    rows8 = coarsen(rows7)
    own5[...] = rows5.reshape(8, 16, 256)
    own6[...] = rows6.reshape(4, 16, 256)
    own7[...] = rows7.reshape(2, 16, 256)
    own8[...] = rows8.reshape(1, 16, 256)

    stage_b = []
    owns = (own5, own6, own7, own8)
    for m in range(15, 0, -1):
        up = m.bit_length() - 1
        count = 8 >> up
        start = 8 * up + (w % 2**up) * count
        copy = remote(
            owns[up], rf.at[pl.ds(start, count)], b_send.at[m - 1], b_recv.at[m - 1],
            place(x, y, flip(w, m, 4)),
        )
        copy.start()
        stage_b.append(copy)

    def unit_forward(unit, other):
        weights, peak, weighted, total = attend(qp[unit], kvp[other])
        w1[unit] = weights
        w1p[unit], w1w[unit], w1t[unit] = peak, weighted, total

    for mask in (1, 3, 2):
        for copy in moves[mask][:2]:
            copy.wait_recv()
        kvp[flip(x, mask, 2)] = coarsen(kvb[flip(x, mask, 2)])
    kvp[4] = coarsen(kvp[0:2].reshape(256, 256))
    kvp[5] = coarsen(kvp[2:4].reshape(256, 256))
    own3[...] = coarsen(kvp[4:6].reshape(256, 256))
    level3 = remote(own3, kv3sib, c_send.at[0], c_recv.at[0], place(x, sib, w))
    level3.start()
    for mask in (1, 3, 2):
        moves[mask][2].wait_recv()
        chunk_forward(flip(x, mask, 2))
        if mask == 1:
            unit_forward(x, flip(x, 1, 2))
            unit_forward(flip(x, 1, 2), x)
    qp[4] = coarsen(qp[0:2].reshape(256, LANES))
    qp[5] = coarsen(qp[2:4].reshape(256, LANES))
    qp[6] = coarsen(qp[4:6].reshape(256, LANES))
    unit_forward(flip(x, 3, 2), flip(x, 2, 2))
    unit_forward(flip(x, 2, 2), flip(x, 3, 2))
    unit_forward(4, 5)
    unit_forward(5, 4)
    level3.wait_recv()
    kvp[7] = kv3sib[...]
    unit_forward(6, 7)

    qs = mm(half, qp[6])
    qs = jnp.concatenate([qs, jnp.zeros((64, LANES), F32)], axis=0)
    shape = (LANES, LANES)
    row, col = iota(shape, 0), iota(shape, 1)
    down = jnp.where((row >= 64) & (shr(col, 1) == row - 64), 0.5, 0.0).astype(BF16)
    qs = qs.astype(BF16)
    upper_rows = iota((LANES, 1), 0) >= 64
    for _ in range(4):
        qs = jnp.where(upper_rows, mm(down, qs), qs.astype(F32)).astype(BF16)
    level = row_level(jnp.bitwise_and(iota((256, 1), 0), 127))

    for copy in stage_b:
        copy.wait_recv()
    far4 = r4[pl.ds(2 * (1 - y_pair), 2)].reshape(LANES, 256)
    far = jnp.concatenate([far4, rf[...].reshape(512, 256)], axis=0)
    far_vals = with_ones(far[:, LANES:])
    q_stack = stack_heads(qs)
    weights_s, peak_s = soft_weights(pick(mm_nt(q_stack, far[:, :LANES]), level))
    blocks_s = blocks_of(weights_s, level)
    both = mm(blocks_s, far_vals)
    weighted_s = fold(both[:, :LANES], LANES)
    total_s = fold(both[:, LANES:], LANES)
    peak_s = fold(jnp.broadcast_to(peak_s, (256, LANES)), LANES)

    spreads = level_spread()
    stats = jnp.concatenate(
        [peak_s.astype(BF16), *split2(weighted_s), *split2(total_s)], axis=1
    )
    taken = [mm(part.astype(BF16), stats) for part in spreads]
    m3 = w1p[6]
    for t in taken:
        m3 = jnp.maximum(m3, t[:, :LANES])
    a3 = jnp.exp(w1p[6] - m3)
    n3, d3 = a3 * w1w[6], a3 * w1t[6]
    shares_s = []
    for index, t in enumerate(taken):
        share = 2.0 ** (index + 1) * jnp.exp(t[:, :LANES] - m3)
        n3 = n3 + share * (t[:, 128:256] + t[:, 256:384])
        d3 = d3 + share * (t[:, 384:512] + t[:, 512:640])
        shares_s.append(share)

    used = [0]

    def fresh():
        used[0] += 1
        return sp.at[used[0] - 1]

    def doubled(values):
        count, ref = values.shape[0], fresh()
        ref[pl.ds(0, count, 2), :] = values
        ref[pl.ds(1, count, 2), :] = values
        return ref[0 : 2 * count, :]

    def paired(values):
        count, ref = values.shape[0], fresh()
        ref[0:count, :] = values
        return ref[pl.ds(0, count // 2, 2), :] + ref[pl.ds(1, count // 2, 2), :]

    def merge(peak, weighted, total, m, n, d):
        crest = jnp.maximum(peak, m)
        own = jnp.exp(peak - crest)
        rest = 2.0 * jnp.exp(m - crest)
        return crest, own * weighted + rest * n, own * total + rest * d, own, rest

    m2, n2, d2, own2, rest2 = merge(
        w1p[4:6].reshape(256, LANES), w1w[4:6].reshape(256, LANES), w1t[4:6].reshape(256, LANES),
        doubled(m3), doubled(n3), doubled(d3),
    )
    crest1, n1v, d1v, own1, rest1 = merge(
        w1p[0:4].reshape(512, LANES), w1w[0:4].reshape(512, LANES), w1t[0:4].reshape(512, LANES),
        doubled(m2), doubled(n2), doubled(d2),
    )
    m1[...] = crest1.reshape(4, LANES, LANES)
    n1[...] = n1v.reshape(4, LANES, LANES)
    d1[...] = d1v.reshape(4, LANES, LANES)

    same = jnp.where(shr(iota(shape, 0), 6) == shr(iota(shape, 1), 6), 1.0, 0.0).astype(BF16)
    head_sum = jnp.concatenate([same, same], axis=0)

    def output_copy(kind, mask):
        px = flip(x, mask, 2)
        if kind == 0:
            src, dst = ob.at[px], out_ref.at[:, lanes(x)]
        elif kind == 1:
            src, dst = oq.at[px], gq_ref.at[:, lanes(x)]
        elif kind == 2:
            src, dst = bk.at[px], bkr.at[x]
        else:
            src, dst = bv.at[px], bvr.at[x]
        return remote(
            src, dst, o_send.at[kind, mask - 1], o_recv.at[kind, mask - 1], place(px, y, w)
        )

    for mask in (1, 3, 2, 0):
        px = flip(x, mask, 2)
        crest, numer, denom, own, rest = merge(
            w0p[px], w0w[px], w0t[px], doubled(m1[px]), doubled(n1[px]), doubled(d1[px])
        )
        inverse = 1.0 / denom
        ratio = numer * inverse
        ob[px] = ratio.astype(BF16)
        ratios[mask], inverses[mask] = ratio, inverse
        w0p[px], w0t[px] = own, rest
    outs = {(kind, mask): output_copy(kind, mask) for kind in range(4) for mask in (1, 3, 2)}
    locals_ = [
        pltpu.make_async_copy(ob.at[x], out_ref.at[:, lanes(x)], loc.at[0]),
        pltpu.make_async_copy(oq.at[x], gq_ref.at[:, lanes(x)], loc.at[1]),
        pltpu.make_async_copy(bk.at[x], bkr.at[x], loc.at[2]),
        pltpu.make_async_copy(cs.at[x], cb.at[x], loc.at[3]),
        pltpu.make_async_copy(bv.at[x], bvr.at[x], loc.at[4]),
    ]
    for mask in (1, 3, 2):
        outs[0, mask].start()
    locals_[0].start()

    loads[5].wait()
    for mask in (0, 1, 3, 2):
        px = flip(x, mask, 2)
        if mask:
            moves[mask][3].wait_recv()
        up = gb[px].astype(F32)
        inverse = inverses[mask]
        high, low = split2(up * ratios[mask])
        drift = -mm(jnp.concatenate([high, low], axis=1), head_sum) * inverse
        scaled = up * inverse
        own, rest = w0p[px], w0t[px]
        gw0[px] = (own * scaled).astype(BF16)
        gt0[px] = own * drift
        g1s[px] = paired(rest * scaled)
        d1s[px] = paired(rest * drift)

    g1, dd1 = g1s[...].reshape(512, LANES), d1s[...].reshape(512, LANES)
    gw1[0:4] = (own1 * g1).astype(BF16).reshape(4, LANES, LANES)
    gt1[0:4] = (own1 * dd1).reshape(4, LANES, LANES)
    g2 = paired(rest1 * g1)
    dd2 = paired(rest1 * dd1)
    gw1[4:6] = (own2 * g2).astype(BF16).reshape(2, LANES, LANES)
    gt1[4:6] = (own2 * dd2).reshape(2, LANES, LANES)
    g3 = paired(rest2 * g2)
    dd3 = paired(rest2 * dd2)
    gw1[6] = (a3 * g3).astype(BF16)
    gt1[6] = a3 * dd3
    pieces = []
    for share in shares_s:
        pieces.append(
            jnp.concatenate([(share * g3).astype(BF16), *split2(share * dd3)], axis=1)
        )
    pooled = mm(level_pool(), jnp.concatenate(pieces, axis=0))
    gw_s = pooled[:, :LANES].astype(BF16)
    gt_s = pooled[:, 128:256] + pooled[:, 256:384]

    grads_s = stack_grads(gw_s, gt_s)
    lift = pick(mm_nt(grads_s, far_vals), level)
    gs = (weights_s.astype(F32) * lift).astype(BF16)
    gs_blocks = blocks_of(gs, level)
    gk_far = mm_tn(gs_blocks, q_stack)
    gv_far = mm_tn(blocks_s, grads_s[:, :LANES])
    far_grads = jnp.concatenate([gk_far, gv_far], axis=1)
    s4[...] = far_grads[:LANES].astype(BF16).reshape(2, 64, 256)
    sb[...] = far_grads[LANES:].astype(BF16).reshape(32, 16, 256)

    back_b = []
    for m in range(15, 0, -1):
        up = m.bit_length() - 1
        count = 8 >> up
        pw = flip(w, m, 4)
        theirs = 8 * up + (pw % 2**up) * count
        ours = 8 * up + (w % 2**up) * count
        copy = remote(
            sb.at[pl.ds(theirs, count)], rb.at[pl.ds(ours, count)],
            bb_send.at[m - 1], bb_recv.at[m - 1], place(x, y, pw),
        )
        copy.start()
        back_b.append(copy)

    gq_s = fold(mm(gs_blocks, far[:, :LANES]), LANES) * 0.125
    high, low = split2(gq_s)
    weighted_spread = spreads[0] * 0.5
    for index in range(1, 5):
        weighted_spread = weighted_spread + spreads[index] * 0.5 ** (index + 1)
    weighted_spread = weighted_spread.astype(BF16)
    run_q3 = mm(weighted_spread, high) + mm(weighted_spread, low)

    for unit in range(6, -1, -1):
        gq1[unit], gkv1[unit ^ 1] = attend_back(
            qp[unit], kvp[unit ^ 1], w1[unit], gw1[unit], gt1[unit]
        )

    s3[...] = gkv1[7].astype(BF16)
    back_y = [remote(s3, e3, ey_send.at[0], ey_recv.at[0], place(x, sib, w))]
    for m in (2, 3):
        py = flip(y, m, 2)
        back_y.append(
            remote(
                s4.at[py % 2], e4.at[y_bit], ey_send.at[m - 1], ey_recv.at[m - 1], place(x, py, w)
            )
        )
    for copy in back_y:
        copy.start()

    run_q2 = gq1[4:6].reshape(256, LANES) + 0.5 * doubled(gq1[6] + run_q3)
    run_q1 = gq1[0:4].reshape(512, LANES) + 0.5 * doubled(run_q2)
    run_k2 = gkv1[4:6, :, :LANES].reshape(256, LANES)
    run_v2 = gkv1[4:6, :, LANES:].reshape(256, LANES)
    run_k1 = gkv1[0:4, :, :LANES].reshape(512, LANES) + 0.5 * doubled(run_k2)
    run_v1 = gkv1[0:4, :, LANES:].reshape(512, LANES) + 0.5 * doubled(run_v2)
    m1[...] = run_q1.reshape(4, LANES, LANES)
    n1[...] = run_k1.reshape(4, LANES, LANES)
    d1[...] = run_v1.reshape(4, LANES, LANES)

    for mask in (1, 3, 2, 0):
        px = flip(x, mask, 2)
        gq, gkv = attend_back(qb[px], kvb[px], w0[px], gw0[px], gt0[px])
        gq = (gq + 0.5 * doubled(m1[px])).astype(BF16)
        gk = (gkv[:, :LANES] + 0.5 * doubled(n1[px])).astype(BF16)
        gv = (gkv[:, LANES:] + 0.5 * doubled(d1[px])).astype(BF16)
        oq[px] = gq
        bk[px] = gk
        bv[px] = gv
        if mask:
            outs[1, mask].start()
            outs[2, mask].start()
            outs[3, mask].start()
    locals_[1].start()
    locals_[2].start()
    locals_[4].start()

    for copy in back_b:
        copy.wait_recv()
    shape = (LANES, LANES)
    row, col = iota(shape, 0), iota(shape, 1)
    gather = []
    for up in range(4):
        inside = jnp.bitwise_and(col, (LANES >> up) - 1)
        gather.append(jnp.where(shr(row, up) == inside, 0.5**up, 0.0))
    gather = jnp.concatenate(gather, axis=1).astype(BF16)
    s5[...] = mm(gather, rb[...].reshape(512, 256)).astype(BF16).reshape(4, 2, 16, 256)
    for m in (1, 2, 3):
        py = flip(y, m, 2)
        copy = remote(s5.at[py], e5.at[y], e5_send.at[m - 1], e5_recv.at[m - 1], place(x, py, w))
        copy.start()
        back_y.append(copy)
    e5[y] = s5[y]
    fill = [jnp.where(row == col, 1.0, 0.0)]
    inside = jnp.bitwise_and(col, 63)
    fill.append(jnp.where(shr(row, 1) == inside, 0.5, 0.0))
    inside = jnp.bitwise_and(col, 31)
    fill.append(jnp.where(shr(row, 2) == inside, 0.25, 0.0))
    fill = jnp.concatenate(fill, axis=1).astype(BF16)
    for copy in back_y:
        copy.wait_recv()
    rows = jnp.concatenate([e3[...], e4[...].reshape(LANES, 256), e5[...].reshape(LANES, 256)], axis=0)
    cs[...] = mm(fill, rows).astype(BF16).reshape(4, 2, 16, 256)
    back_x = []
    for m in (1, 3, 2):
        px = flip(x, m, 2)
        copy = remote(cs.at[px], cb.at[x], cx_send.at[m - 1], cx_recv.at[m - 1], place(px, y, w))
        copy.start()
        back_x.append(copy)
    locals_[3].start()

    for copy in back_x:
        copy.wait_recv()
    for copy in outs.values():
        copy.wait_recv()
    for copy in locals_:
        copy.wait()
    for copies in (
        stage_a, [level3], stage_b, back_b, back_y, back_x, outs.values(),
        *moves.values(),
    ):
        for copy in copies:
            copy.wait_send()


def finish(out_v, gq_v, cb, bk, bv, out_ref, gq_ref, gk_ref, gv_ref, gk_v, gv_v, sems):
    writes = [
        pltpu.make_async_copy(out_v, out_ref, sems.at[0]),
        pltpu.make_async_copy(gq_v, gq_ref, sems.at[1]),
    ]
    for copy in writes:
        copy.start()
    shape = (256, 32)
    last = jnp.where(shr(iota(shape, 0), 3) == iota(shape, 1), 0.125, 0.0).astype(BF16)
    for j in range(4):
        total = mm(last, cb[j].reshape(32, 256))
        gk_v[:, j * LANES : (j + 1) * LANES] = (total[:, :LANES] + bk[j].astype(F32)).astype(BF16)
        gv_v[:, j * LANES : (j + 1) * LANES] = (total[:, LANES:] + bv[j].astype(F32)).astype(BF16)
    for i, (src, dst) in enumerate(((gk_v, gk_ref), (gv_v, gv_ref))):
        copy = pltpu.make_async_copy(src, dst, sems.at[2 + i])
        copy.start()
        writes.append(copy)
    for copy in writes:
        copy.wait()


def shards(query, key_in, value_in, grad_out):
    rows, width = query.shape
    whole = jax.ShapeDtypeStruct((rows, width), BF16)

    def f32(*shape):
        return pltpu.VMEM(shape, F32)

    def b16(*shape):
        return pltpu.VMEM(shape, BF16)

    dma = pltpu.SemaphoreType.DMA
    scratch = [
        b16(256, 512), b16(256, 512),
        b16(4, 256, 128), b16(4, 256, 256), b16(4, 256, 128),
        b16(4, 16, 256), b16(128, 256), b16(128, 256), b16(4, 4, 16, 256),
        b16(8, 16, 256), b16(4, 16, 256), b16(2, 16, 256), b16(1, 16, 256),
        b16(32, 16, 256),
        b16(7, 128, 128), b16(8, 128, 256),
        b16(4, 512, 256), b16(7, 256, 128),
        f32(4, 256, 128), f32(4, 256, 128), f32(4, 256, 128),
        f32(7, 128, 128), f32(7, 128, 128), f32(7, 128, 128),
        f32(4, 128, 128), f32(4, 128, 128), f32(4, 128, 128),
        b16(4, 256, 128), f32(4, 256, 128), b16(7, 128, 128), f32(7, 128, 128),
        f32(48, 512, 128), f32(4, 128, 128), f32(4, 128, 128),
        b16(4, 256, 128), b16(4, 256, 128), b16(4, 256, 128), b16(4, 256, 128),
        f32(7, 128, 128), f32(8, 128, 256),
        b16(32, 16, 256), b16(32, 16, 256),
        b16(128, 256), b16(2, 64, 256), b16(4, 2, 16, 256),
        b16(128, 256), b16(2, 64, 256), b16(4, 2, 16, 256),
        b16(4, 2, 16, 256), f32(4, 256, 128), f32(4, 256, 128),
        dma((4, 3)), dma((4, 3)), dma((15,)), dma((15,)),
        dma((1,)), dma((1,)), dma((15,)), dma((15,)), dma((15,)), dma((15,)),
        dma((3,)), dma((3,)), dma((3,)), dma((3,)), dma((3,)), dma((3,)),
        dma((4, 3)), dma((4, 3)), dma((6,)),
    ]
    hbm = pl.BlockSpec(memory_space=pltpu.HBM)
    vmem = pl.BlockSpec(memory_space=pltpu.VMEM)
    anywhere = pl.BlockSpec(memory_space=pl.ANY)
    parts = pl.pallas_call(
        kernel,
        out_shape=(
            whole, whole,
            jax.ShapeDtypeStruct((4, 2, 16, 256), BF16), *[jax.ShapeDtypeStruct((4, 256, 128), BF16)] * 2,
        ),
        in_specs=[hbm] * 4,
        out_specs=(anywhere,) * 5,
        scratch_shapes=scratch,
        compiler_params=pltpu.CompilerParams(
            collective_id=0, has_side_effects=True, vmem_limit_bytes=54036 * 2**10
        ),
    )(query, key_in, value_in, grad_out)
    return pl.pallas_call(
        finish,
        out_shape=(whole,) * 4,
        in_specs=[vmem] * 5,
        out_specs=(hbm,) * 4,
        scratch_shapes=[b16(256, 512), b16(256, 512), dma((4,))],
        compiler_params=pltpu.CompilerParams(vmem_limit_bytes=8 * 2**20),
    )(*parts)


def solution(mesh):
    spec = P(("grp", "seq"), None)
    return jax.shard_map(
        shards, mesh=mesh, in_specs=(spec,) * 4, out_specs=(spec,) * 4, check_vma=False
    )
```
